512 devices in a mesh: frames: 8 (over x, core), atoms: 64 (over z, y).
Axes of the slice: x: 4, y: 8, z: 8, core: 2. Of those that a mesh axis runs over, the one named last changes fastest.
Arguments:
- coords: bfloat16 [8, 3, 4194304], P('frames', None, 'atoms'), may hold values from -32 to 32, as said below
- reference_structure: float32 [3, 4194304], P(None, 'atoms'), may hold values from -8 to 8
Outputs:
- mean_structure: float32 [3, 4194304], P(None, 'atoms')
- transforms: float32 [8, 12], P('frames')
The draws below stay inside these ranges and needn't reach their ends.
Inputs may be any that keep to these rules, and one draw needn't show every extreme that they name: `coords`: every frame is a perturbed affine image of one common structure plus independent per-atom displacements.
All inputs are finite; a program needn't handle non-finite values.
Results may differ from the reference program's by a relative error of at most 0.0003.
Values may be sent and summed in bfloat16 or wider, within the bound.
A program may use at most 128 MiB of HBM per device.

```python
import jax
import jax.numpy as jnp
from jax import lax

ITERS = 2
ATOMS = 4194304
FRAMES = 8


def common_skeleton(key):
    raw = jnp.clip(jax.random.normal(jax.random.fold_in(key, 0), (3, ATOMS), jnp.float32), -2.8, 2.8)
    position = jnp.arange(ATOMS, dtype=jnp.float32) / ATOMS
    growth = 0.7 * jnp.exp(position * 1.0986123)
    return raw * growth[None, :] + position[None, :]


def draw_coords(key, part):
    skeleton = common_skeleton(key)
    key = jax.random.fold_in(key, 11)
    key_mix, key_offset, key_jitter = jax.random.split(key, 3)
    mixing = jnp.eye(3, dtype=jnp.float32)[None] + 0.3 * jnp.clip(jax.random.normal(key_mix, (FRAMES, 3, 3), jnp.float32), -3.0, 3.0)
    offset = jnp.clip(jax.random.normal(key_offset, (FRAMES, 3, 1), jnp.float32), -3.0, 3.0)
    jitter = 1.2 * jnp.clip(jax.random.normal(key_jitter, (FRAMES, 3, ATOMS), jnp.float32), -3.0, 3.0)
    moved = mixing[:, :, 0, None] * skeleton[None, 0:1, :]
    moved = moved + mixing[:, :, 1, None] * skeleton[None, 1:2, :]
    moved = moved + mixing[:, :, 2, None] * skeleton[None, 2:3, :]
    return jnp.clip(moved + offset + jitter, -32.0, 32.0).astype(jnp.bfloat16)


def draw_reference_structure(key, part):
    skeleton = common_skeleton(key)
    key = jax.random.fold_in(key, 23)
    jitter = 0.3 * jnp.clip(jax.random.normal(key, (3, ATOMS), jnp.float32), -3.0, 3.0)
    return skeleton + jitter


def setup_inputs(seed: int = 0) -> dict:
    keys = jax.random.split(jax.random.key(seed), 3)
    return {
        "coords": draw_coords(jax.random.fold_in(keys[2], 71), 0),
        "reference_structure": draw_reference_structure(jax.random.fold_in(keys[2], 71), 0),
    }


highest = lax.Precision.HIGHEST
eps = 1e-06

def augment_one(single_frame):
    values = single_frame.astype(jnp.float32)
    unit_row = jnp.ones_like(values[:1])
    return jnp.concatenate([values, unit_row], axis=0)

def solve_one(cross, gram):
    factor = jnp.linalg.cholesky(gram)
    return jax.scipy.linalg.cho_solve((factor, True), cross.T).T

def reference(coords, reference_structure):
    frame_count = coords.shape[0]
    atom_count = coords.shape[2]

    def gram_one(single_frame):
        augmented = augment_one(single_frame)
        return jnp.dot(augmented, augmented.T, precision=highest)
    grams = lax.map(gram_one, coords)
    structure = reference_structure
    affine_maps = jnp.zeros((frame_count, 3, 4), jnp.float32)
    for step in range(ITERS):

        def cross_one(single_frame):
            return jnp.dot(structure, augment_one(single_frame).T, precision=highest)
        crosses = lax.map(cross_one, coords)
        affine_maps = jax.vmap(solve_one)(crosses, grams)

        def accumulate(running, carried):
            single_frame, affine_one = carried
            return (running + jnp.dot(affine_one, augment_one(single_frame), precision=highest), None)
        summed, _ = lax.scan(accumulate, jnp.zeros((3, atom_count), jnp.float32), (coords, affine_maps))
        mean_raw = summed / frame_count
        centre = lax.optimization_barrier(jnp.sum(mean_raw, axis=1)) / atom_count
        shifted = mean_raw - centre[:, None]
        spread = jnp.sqrt(jnp.sum(shifted * shifted) / atom_count + eps)
        structure = shifted / spread
    return (structure, affine_maps.reshape(frame_count, 12))
```

```python
import functools

import jax
import jax.numpy as jnp
from jax import lax
from jax.experimental import pallas as pl
from jax.experimental.pallas import tpu as pltpu
from jax.sharding import PartitionSpec as P

MESH = pl.DeviceIdType.MESH
F32, BF16 = jnp.float32, jnp.bfloat16
eps = 1e-06
FRAMES = 8
CHUNKS = 16
OFFSETS = ((2, 0), (2, 1), (1, 0), (1, 1), (3, 0), (3, 1), (0, 1), (0, 0))


def iota(shape, dim):
    return lax.broadcasted_iota(jnp.int32, shape, dim)


def split3(value):
    high = value.astype(BF16)
    rest = value - high.astype(F32)
    middle = rest.astype(BF16)
    low = (rest - middle.astype(F32)).astype(BF16)
    return high, middle, low


def kernel(ny, nz, coords, start, out, maps, xin, rin, tmp, packed, z, sums, piece,
           in_sem, send1, recv1, send2, recv2, send3, recv3, own_sem):
    frame = lax.axis_index("frames")
    block = lax.axis_index("atoms")
    x, core = frame // 2, frame % 2
    row, col = block // ny, block % ny
    share = rin.shape[1]
    tiles = share // 128
    width = share // CHUNKS
    lane_tiles = width // 128
    atom_count = float(share * FRAMES * ny * nz)

    def frame_at(k):
        dx, dc = OFFSETS[k]
        return lax.rem(x + dx, 4) * 2 + lax.rem(core + dc, 2)

    def columns(index):
        return pl.ds(pl.multiple_of(index * share, share), share)

    loads = []
    for k in range(FRAMES):
        loads.append(pltpu.make_async_copy(
            coords.at[0, :, columns(frame_at(k))], xin.at[k], in_sem.at[k]))
        loads[-1].start()
    load_start = pltpu.make_async_copy(start.at[:, columns(frame)], rin, in_sem.at[FRAMES])
    load_start.start()

    barrier = pltpu.get_barrier_semaphore()
    for k in range(FRAMES - 1):
        pl.semaphore_signal(barrier, inc=1, device_id=(frame_at(k), block), device_id_type=MESH)
    for d in range(1, ny):
        pl.semaphore_signal(
            barrier, inc=1, device_id=(frame, row * ny + lax.rem(col + d, ny)), device_id_type=MESH)
    for d in range(1, nz):
        pl.semaphore_signal(
            barrier, inc=1, device_id=(frame, lax.rem(row + d, nz) * ny + col), device_id_type=MESH)

    def spread_tiles(load):
        for t in range(tiles):
            tmp[4 * t:4 * t + 3, :] = load(t)

    def dense(j, q):
        return tmp[pl.ds(j + 4 * CHUNKS * q, CHUNKS, stride=4), :]

    own_rows = pl.ds(pl.multiple_of(frame * 3 * CHUNKS, 3 * CHUNKS), 3 * CHUNKS)
    exchange = []
    for k in range(FRAMES):
        loads[k].wait()
        spread_tiles(lambda t: xin[k, :, 128 * t:128 * (t + 1)].astype(F32))
        for j in range(3):
            for q in range(lane_tiles):
                packed[k, CHUNKS * j:CHUNKS * (j + 1), 128 * q:128 * (q + 1)] = dense(j, q).astype(BF16)
        if k == 0:
            pl.semaphore_wait(barrier, FRAMES - 1 + ny - 1 + nz - 1)
        if k < FRAMES - 1:
            exchange.append(pltpu.make_async_remote_copy(
                packed.at[k], z.at[own_rows], send1.at[k], recv1.at[k],
                device_id=(frame_at(k), block), device_id_type=MESH))
            exchange[-1].start()
    own = pltpu.make_async_copy(packed.at[FRAMES - 1], z.at[own_rows], own_sem.at[0])
    own.start()

    coord_rows = 3 * FRAMES * CHUNKS
    z[coord_rows:coord_rows + CHUNKS, :] = jnp.ones((CHUNKS, width), BF16)
    z[coord_rows + 7 * CHUNKS:coord_rows + 8 * CHUNKS, :] = jnp.zeros((CHUNKS, width), BF16)
    load_start.wait()
    spread_tiles(lambda t: rin[:, 128 * t:128 * (t + 1)])
    for j in range(3):
        for q in range(lane_tiles):
            value = dense(j, q)
            high = value.astype(BF16)
            low = (value - high.astype(F32)).astype(BF16)
            at = coord_rows + CHUNKS * (1 + j)
            z[at:at + CHUNKS, 128 * q:128 * (q + 1)] = high
            z[at + 3 * CHUNKS:at + 4 * CHUNKS, 128 * q:128 * (q + 1)] = low

    total_rows = coord_rows + 8 * CHUNKS
    group = iota((total_rows, 128), 0) >> 4
    place = jnp.where(group == 3 * FRAMES, group, (group % 3) * FRAMES + group // 3)
    collect = jnp.where(
        (place == iota((total_rows, 128), 1)) & (group <= 3 * FRAMES), 1.0, 0.0).astype(BF16)
    same_chunk = iota((CHUNKS, total_rows), 0) == (iota((CHUNKS, total_rows), 1) & (CHUNKS - 1))
    sub = iota((8, 128), 0)
    lane = iota((8, 128), 1)

    own.wait()
    for k in range(FRAMES - 1):
        exchange[k].wait_recv()

    groups = 3 * FRAMES + 7
    gram = lax.dot_general(
        z[0:groups * CHUNKS, :], z[...], (((1,), (1,)), ((), ())), preferred_element_type=F32)
    gram = jnp.where(same_chunk[None], gram.reshape(groups, CHUNKS, total_rows), 0.0)
    gram = (gram[:, :8] + gram[:, 8:]).reshape(groups * 8, total_rows)
    gram = sum(jnp.dot(part, collect, preferred_element_type=F32) for part in split3(gram))
    gram = gram.reshape(groups, 8, 128)

    def moment_row(g):
        return jnp.sum(gram[g], axis=0, keepdims=True)

    moments = jnp.zeros((8, 128), F32)
    for j in range(3):
        rows_j = jnp.zeros((8, 128), F32)
        for f in range(FRAMES):
            rows_j = jnp.where(sub == f, moment_row(3 * f + j), rows_j)
        moments = moments + (pltpu.roll(rows_j, 32 * j, 1) if j else rows_j)
    rows_3 = jnp.zeros((8, 128), F32)
    for a in range(3):
        rows_3 = jnp.where(
            (sub & 3) == a, moment_row(3 * FRAMES + 1 + a) + moment_row(3 * FRAMES + 4 + a), rows_3)
    rows_3 = jnp.where((sub & 3) == 3, moment_row(3 * FRAMES), rows_3)
    moments = moments + pltpu.roll(rows_3, 96, 1)

    sends = []
    stages = (
        (FRAMES, frame, lambda d: (lax.rem(frame + d, FRAMES), block)),
        (ny, col, lambda d: (frame, row * ny + lax.rem(col + d, ny))),
        (nz, row, lambda d: (frame, lax.rem(row + d, nz) * ny + col)),
    )
    for stage, (size, me, partner) in enumerate(stages):
        if size == 1:
            continue
        sums[stage, me] = moments
        copies = []
        for d in range(1, size):
            copies.append(pltpu.make_async_remote_copy(
                sums.at[stage, me], sums.at[stage, me], send2.at[stage, d], recv2.at[stage, d],
                device_id=partner(d), device_id_type=MESH))
            copies[-1].start()
        for copy in copies:
            copy.wait_recv()
        sends += copies
        moments = sums[stage, 0]
        for s in range(1, size):
            moments = moments + sums[stage, s]

    inside = lane < 3 * FRAMES + 1
    r = [jnp.where(inside, moments if j == 0 else pltpu.roll(moments, 128 - 32 * j, 1), 0.0) for j in range(4)]
    mean_row = r[3][3:4, :] * (1.0 / atom_count)
    at = 3 * FRAMES
    centred = [v - v[:, at:at + 1] * mean_row for v in r]

    def block_of(value, i):
        return value if i == 0 else pltpu.roll(value, 128 - FRAMES * i, 1)

    diagonal = (lane & (FRAMES - 1)) == sub
    gd = [jnp.broadcast_to(jnp.sum(jnp.where(diagonal, centred[j], 0.0), axis=0, keepdims=True), (8, 128))
          for j in range(3)]
    first = lane < FRAMES
    one = jnp.ones((8, 128), F32)
    g00, g11, g22 = (jnp.where(first, block_of(gd[j], j), one) for j in range(3))
    g01, g02, g12 = (jnp.where(first, v, 0.0) for v in (block_of(gd[0], 1), block_of(gd[0], 2), block_of(gd[1], 2)))
    i0 = 1.0 / g00
    l10, l20 = g01 * i0, g02 * i0
    i1 = 1.0 / (g11 - l10 * g01)
    t12 = g12 - l20 * g01
    l21 = t12 * i1
    i2 = 1.0 / (g22 - l20 * g02 - l21 * t12)

    def solve(c):
        y0 = c[0]
        y1 = c[1] - l10 * y0
        y2 = c[2] - l20 * y0 - l21 * y1
        x2 = y2 * i2
        x1 = y1 * i1 - l21 * x2
        x0 = y0 * i0 - l10 * x1 - l20 * x2
        return [x0, x1, x2]

    def blocks(value):
        return [jnp.where(first, block_of(value, i), 0.0) for i in range(3)]

    def cross(maps_t):
        parts = []
        for j in range(3):
            total = None
            for f in range(FRAMES):
                term = maps_t[j][:, f:f + 1] * centred[j][f:f + 1, :]
                total = term if total is None else total + term
            parts.append(total)
        return blocks(parts[0] + parts[1] + parts[2])

    used = (sub < 3) & first

    def square_mean(maps_t, crosses):
        value = sum(m * c for m, c in zip(maps_t, crosses))
        value = jnp.sum(jnp.where(used, value, 0.0), axis=0, keepdims=True)
        return jnp.sum(value, axis=1, keepdims=True) * (1.0 / atom_count)

    share_of = 1.0 / FRAMES
    m1 = [v * share_of for v in solve(blocks(centred[3]))]
    c1 = cross(m1)
    m2 = [v * share_of for v in solve(c1)]
    c2 = cross(m2)
    variance1 = square_mean(m1, c1) + eps
    variance2 = square_mean(m2, c2) + eps * variance1
    scale = 1.0 / jnp.sqrt(variance2)

    mean_blocks = blocks(jnp.broadcast_to(mean_row, (8, 128)))
    shift = -sum(m * v for m, v in zip(m2, mean_blocks))
    offset = jnp.sum(shift, axis=1, keepdims=True) * scale

    joined = m2[0] + pltpu.roll(m2[1], FRAMES, 1) + pltpu.roll(m2[2], 2 * FRAMES, 1)
    stacked = jnp.concatenate([v.astype(F32) for v in split3(joined)], axis=0).astype(BF16)
    source = iota((128, coord_rows), 1) >> 4
    expand = jnp.where((source % 3) * FRAMES + source // 3 == iota((128, coord_rows), 0), 1.0, 0.0).astype(BF16)
    wide = jnp.dot(stacked, expand, preferred_element_type=F32)
    chunk = iota((8, coord_rows), 1) & (CHUNKS - 1)
    half = iota((8, coord_rows), 0) >> 2
    lhs = jnp.concatenate(
        [jnp.where(chunk == half + 2 * rg, wide[8 * s:8 * s + 8], 0.0) for s in range(3) for rg in range(8)],
        axis=0).astype(BF16)
    aligned = jnp.dot(lhs, z[0:coord_rows, :], preferred_element_type=F32)
    aligned = aligned[0:64] + aligned[64:128] + aligned[128:192]
    for rg in range(8):
        value = aligned[8 * rg:8 * rg + 8] * scale + offset
        for h in range(2):
            for q in range(lane_tiles):
                t = q * CHUNKS + 2 * rg + h
                piece[:, 128 * t:128 * (t + 1)] = value[4 * h:4 * h + 3, 128 * q:128 * (q + 1)]

    own = pltpu.make_async_copy(piece, out.at[:, columns(frame)], own_sem.at[1])
    own.start()
    gather = []
    for k in range(FRAMES - 1):
        gather.append(pltpu.make_async_remote_copy(
            piece, out.at[:, columns(frame)], send3.at[k], recv3.at[k],
            device_id=(frame_at(k), block), device_id_type=MESH))
        gather[-1].start()

    back = FRAMES / jnp.sqrt(variance1)
    entries = [m * back for m in m2] + [shift * back]
    line = jnp.zeros((8, 128), F32)
    for j in range(4):
        value = jnp.sum(jnp.where(lane == frame, entries[j], 0.0), axis=1, keepdims=True)
        line = jnp.where((lane == 4 * sub + j) & (sub < 3), value, line)
    maps[...] = jnp.sum(line, axis=0, keepdims=True)[:, 0:12]

    own.wait()
    for copy in gather:
        copy.wait_recv()
    for copy in exchange + sends + gather:
        copy.wait_send()


def solution(mesh):
    blocks = mesh.shape["atoms"]
    ny = min(8, blocks)
    nz = blocks // ny

    def per_device(coords, start):
        atoms = start.shape[1]
        share = atoms // FRAMES
        width = share // CHUNKS
        dma = pltpu.SemaphoreType.DMA
        return pl.pallas_call(
            functools.partial(kernel, ny, nz),
            out_shape=(
                jax.ShapeDtypeStruct((3, atoms), F32),
                jax.ShapeDtypeStruct((1, 12), F32),
            ),
            in_specs=[pl.BlockSpec(memory_space=pl.ANY)] * 2,
            out_specs=(
                pl.BlockSpec(memory_space=pl.ANY),
                pl.BlockSpec(memory_space=pltpu.VMEM),
            ),
            scratch_shapes=[
                pltpu.VMEM((FRAMES, 3, share), BF16),
                pltpu.VMEM((3, share), F32),
                pltpu.VMEM((4 * (share // 128), 128), F32),
                pltpu.VMEM((FRAMES, 3 * CHUNKS, width), BF16),
                pltpu.VMEM((32 * CHUNKS, width), BF16),
                pltpu.VMEM((3, 8, 8, 128), F32),
                pltpu.VMEM((3, share), F32),
                dma((FRAMES + 1,)),
                dma((FRAMES - 1,)),
                dma((FRAMES - 1,)),
                dma((3, 8)),
                dma((3, 8)),
                dma((FRAMES - 1,)),
                dma((FRAMES - 1,)),
                dma((2,)),
            ],
            compiler_params=pltpu.CompilerParams(
                collective_id=0, has_side_effects=True, vmem_limit_bytes=32 * 1024 * 1024
            ),
        )(coords, start)

    return jax.shard_map(
        per_device,
        mesh=mesh,
        in_specs=(P("frames", None, "atoms"), P(None, "atoms")),
        out_specs=(P(None, "atoms"), P("frames", None)),
        check_vma=False,
    )
```

```python
import functools

import jax
import jax.numpy as jnp
from jax import lax
from jax.experimental import pallas as pl
from jax.experimental.pallas import tpu as pltpu
from jax.sharding import PartitionSpec as P

MESH = pl.DeviceIdType.MESH
F32, BF16 = jnp.float32, jnp.bfloat16
eps = 1e-06
FRAMES = 8
CHUNKS = 16
OFFSETS = ((2, 0), (2, 1), (1, 0), (1, 1), (3, 0), (3, 1), (0, 1), (0, 0))


def iota(shape, dim):
    return lax.broadcasted_iota(jnp.int32, shape, dim)


def split3(value):
    high = value.astype(BF16)
    rest = value - high.astype(F32)
    middle = rest.astype(BF16)
    low = (rest - middle.astype(F32)).astype(BF16)
    return high, middle, low


def kernel(ny, nz, coords, start, out, maps, xin, rin, tmp, packed, z, others, sums, piece,
           in_sem, send1, recv1, send2, recv2, send3, recv3, send4, recv4, own_sem, out_sem):
    frame = lax.axis_index("frames")
    block = lax.axis_index("atoms")
    x, core = frame // 2, frame % 2
    row, col = block // ny, block % ny
    share = rin.shape[1]
    tiles = share // 128
    width = share // CHUNKS
    lane_tiles = width // 128
    atom_count = float(share * FRAMES * ny * nz)

    def frame_at(k):
        dx, dc = OFFSETS[k]
        return lax.rem(x + dx, 4) * 2 + lax.rem(core + dc, 2)

    def columns(index):
        return pl.ds(pl.multiple_of(index * share, share), share)

    barrier = pltpu.get_barrier_semaphore()
    for k in range(FRAMES - 1):
        pl.semaphore_signal(barrier, inc=1, device_id=(frame_at(k), block), device_id_type=MESH)
    for d in range(1, ny):
        pl.semaphore_signal(
            barrier, inc=1, device_id=(frame, row * ny + lax.rem(col + d, ny)), device_id_type=MESH)
    for d in range(1, nz):
        pl.semaphore_signal(
            barrier, inc=1, device_id=(frame, lax.rem(row + d, nz) * ny + col), device_id_type=MESH)

    loads = []
    for k in range(FRAMES):
        loads.append(pltpu.make_async_copy(
            coords.at[0, :, columns(frame_at(k))], xin.at[k], in_sem.at[k]))
        loads[-1].start()
    load_start = pltpu.make_async_copy(start.at[:, columns(frame)], rin, in_sem.at[FRAMES])
    load_start.start()

    def spread_tiles(load):
        for t in range(tiles):
            tmp[4 * t:4 * t + 3, :] = load(t)

    def dense(j, q):
        return tmp[pl.ds(j + 4 * CHUNKS * q, CHUNKS, stride=4), :]

    own_rows = pl.ds(pl.multiple_of(frame * 3 * CHUNKS, 3 * CHUNKS), 3 * CHUNKS)
    exchange = []
    for k in range(FRAMES):
        loads[k].wait()
        spread_tiles(lambda t: xin[k, :, 128 * t:128 * (t + 1)].astype(F32))
        for j in range(3):
            for q in range(lane_tiles):
                packed[frame_at(k), CHUNKS * j:CHUNKS * (j + 1), 128 * q:128 * (q + 1)] = dense(j, q).astype(BF16)
        if k == 0:
            pl.semaphore_wait(barrier, FRAMES - 1 + ny - 1 + nz - 1)
        if k < FRAMES - 1:
            exchange.append(pltpu.make_async_remote_copy(
                packed.at[frame_at(k)], z.at[own_rows], send1.at[k], recv1.at[k],
                device_id=(frame_at(k), block), device_id_type=MESH))
            exchange[-1].start()
    own = [pltpu.make_async_copy(packed.at[frame], z.at[own_rows], own_sem.at[0])]
    for m in range(1, 4):
        own.append(pltpu.make_async_copy(
            packed.at[lax.rem(x + m, 4) * 2 + core], others.at[m - 1, own_rows], own_sem.at[m]))
    for copy in own:
        copy.start()

    coord_rows = 3 * FRAMES * CHUNKS
    z[coord_rows:coord_rows + CHUNKS, :] = jnp.ones((CHUNKS, width), BF16)
    z[coord_rows + 7 * CHUNKS:coord_rows + 8 * CHUNKS, :] = jnp.zeros((CHUNKS, width), BF16)
    load_start.wait()
    spread_tiles(lambda t: rin[:, 128 * t:128 * (t + 1)])
    for j in range(3):
        for q in range(lane_tiles):
            value = dense(j, q)
            high = value.astype(BF16)
            low = (value - high.astype(F32)).astype(BF16)
            at = coord_rows + CHUNKS * (1 + j)
            z[at:at + CHUNKS, 128 * q:128 * (q + 1)] = high
            z[at + 3 * CHUNKS:at + 4 * CHUNKS, 128 * q:128 * (q + 1)] = low

    total_rows = coord_rows + 8 * CHUNKS
    group = iota((total_rows, 128), 0) >> 4
    place = jnp.where(group == 3 * FRAMES, group, (group % 3) * FRAMES + group // 3)
    collect = jnp.where(
        (place == iota((total_rows, 128), 1)) & (group <= 3 * FRAMES), 1.0, 0.0).astype(BF16)
    same_chunk = iota((CHUNKS, total_rows), 0) == (iota((CHUNKS, total_rows), 1) & (CHUNKS - 1))
    sub = iota((8, 128), 0)
    lane = iota((8, 128), 1)

    own[0].wait()
    for k in range(FRAMES - 1):
        exchange[k].wait_recv()

    groups = 3 * FRAMES + 7
    gram = lax.dot_general(
        z[0:groups * CHUNKS, :], z[...], (((1,), (1,)), ((), ())), preferred_element_type=F32)
    gram = jnp.where(same_chunk[None], gram.reshape(groups, CHUNKS, total_rows), 0.0)
    gram = (gram[:, :8] + gram[:, 8:]).reshape(groups * 8, total_rows)
    gram = sum(jnp.dot(part, collect, preferred_element_type=F32) for part in split3(gram))
    gram = gram.reshape(groups, 8, 128)

    def moment_row(g):
        return jnp.sum(gram[g], axis=0, keepdims=True)

    moments = jnp.zeros((8, 128), F32)
    for j in range(3):
        rows_j = jnp.zeros((8, 128), F32)
        for f in range(FRAMES):
            rows_j = jnp.where(sub == f, moment_row(3 * f + j), rows_j)
        moments = moments + (pltpu.roll(rows_j, 32 * j, 1) if j else rows_j)
    rows_3 = jnp.zeros((8, 128), F32)
    for a in range(3):
        rows_3 = jnp.where(
            (sub & 3) == a, moment_row(3 * FRAMES + 1 + a) + moment_row(3 * FRAMES + 4 + a), rows_3)
    rows_3 = jnp.where((sub & 3) == 3, moment_row(3 * FRAMES), rows_3)
    moments = moments + pltpu.roll(rows_3, 96, 1)

    sends = []
    def far_first(size):
        return sorted(range(1, size), key=lambda d: -min(d, size - d))

    stages = (
        (FRAMES, frame, range(FRAMES - 1), lambda d: (frame_at(d), block)),
        (ny, col, far_first(ny), lambda d: (frame, row * ny + lax.rem(col + d, ny))),
        (nz, row, far_first(nz), lambda d: (frame, lax.rem(row + d, nz) * ny + col)),
    )
    rest = []
    for stage, (size, me, order, partner) in enumerate(stages):
        if size == 1:
            continue
        sums[stage, me] = moments
        copies = []
        for d in order:
            copies.append(pltpu.make_async_remote_copy(
                sums.at[stage, me], sums.at[stage, me], send2.at[stage, d], recv2.at[stage, d],
                device_id=partner(d), device_id_type=MESH))
            copies[-1].start()
        if stage == 0:
            for m in range(1, 4):
                rest.append([])
                for k in range(FRAMES - 1):
                    to = frame_at(k)
                    rest[-1].append(pltpu.make_async_remote_copy(
                        packed.at[lax.rem(to // 2 + m, 4) * 2 + to % 2], others.at[m - 1, own_rows],
                        send3.at[m - 1, k], recv3.at[m - 1, k], device_id=(to, block), device_id_type=MESH))
                    rest[-1][-1].start()
        for copy in copies:
            copy.wait_recv()
        sends += copies
        moments = sums[stage, 0]
        for s in range(1, size):
            moments = moments + sums[stage, s]

    inside = lane < 3 * FRAMES + 1
    r = [jnp.where(inside, moments if j == 0 else pltpu.roll(moments, 128 - 32 * j, 1), 0.0) for j in range(4)]
    mean_row = r[3][3:4, :] * (1.0 / atom_count)
    at = 3 * FRAMES
    centred = [v - v[:, at:at + 1] * mean_row for v in r]

    def block_of(value, i):
        return value if i == 0 else pltpu.roll(value, 128 - FRAMES * i, 1)

    diagonal = (lane & (FRAMES - 1)) == sub
    gd = [jnp.broadcast_to(jnp.sum(jnp.where(diagonal, centred[j], 0.0), axis=0, keepdims=True), (8, 128))
          for j in range(3)]
    first = lane < FRAMES
    one = jnp.ones((8, 128), F32)
    g00, g11, g22 = (jnp.where(first, block_of(gd[j], j), one) for j in range(3))
    g01, g02, g12 = (jnp.where(first, v, 0.0) for v in (block_of(gd[0], 1), block_of(gd[0], 2), block_of(gd[1], 2)))
    i0 = 1.0 / g00
    l10, l20 = g01 * i0, g02 * i0
    i1 = 1.0 / (g11 - l10 * g01)
    t12 = g12 - l20 * g01
    l21 = t12 * i1
    i2 = 1.0 / (g22 - l20 * g02 - l21 * t12)

    def solve(c):
        y0 = c[0]
        y1 = c[1] - l10 * y0
        y2 = c[2] - l20 * y0 - l21 * y1
        x2 = y2 * i2
        x1 = y1 * i1 - l21 * x2
        x0 = y0 * i0 - l10 * x1 - l20 * x2
        return [x0, x1, x2]

    def blocks(value):
        return [jnp.where(first, block_of(value, i), 0.0) for i in range(3)]

    def cross(maps_t):
        parts = []
        for j in range(3):
            total = None
            for f in range(FRAMES):
                term = maps_t[j][:, f:f + 1] * centred[j][f:f + 1, :]
                total = term if total is None else total + term
            parts.append(total)
        return blocks(parts[0] + parts[1] + parts[2])

    used = (sub < 3) & first

    def square_mean(maps_t, crosses):
        value = sum(m * c for m, c in zip(maps_t, crosses))
        value = jnp.sum(jnp.where(used, value, 0.0), axis=0, keepdims=True)
        return jnp.sum(value, axis=1, keepdims=True) * (1.0 / atom_count)

    share_of = 1.0 / FRAMES
    m1 = [v * share_of for v in solve(blocks(centred[3]))]
    c1 = cross(m1)
    m2 = [v * share_of for v in solve(c1)]
    c2 = cross(m2)
    variance1 = square_mean(m1, c1) + eps
    variance2 = square_mean(m2, c2) + eps * variance1
    scale = 1.0 / jnp.sqrt(variance2)

    mean_blocks = blocks(jnp.broadcast_to(mean_row, (8, 128)))
    shift = -sum(m * v for m, v in zip(m2, mean_blocks))
    offset = jnp.sum(shift, axis=1, keepdims=True) * scale

    joined = m2[0] + pltpu.roll(m2[1], FRAMES, 1) + pltpu.roll(m2[2], 2 * FRAMES, 1)
    stacked = jnp.concatenate([v.astype(F32) for v in split3(joined)], axis=0).astype(BF16)
    source = iota((128, coord_rows), 1) >> 4
    expand = jnp.where((source % 3) * FRAMES + source // 3 == iota((128, coord_rows), 0), 1.0, 0.0).astype(BF16)
    wide = jnp.dot(stacked, expand, preferred_element_type=F32)
    chunk = iota((8, coord_rows), 1) & (CHUNKS - 1)
    half = iota((8, coord_rows), 0) >> 2
    lhs = jnp.concatenate(
        [jnp.where(chunk == half + 2 * rg, wide[8 * s:8 * s + 8], 0.0) for s in range(3) for rg in range(8)],
        axis=0).astype(BF16)
    placed = []

    def finish(m, data):
        aligned = jnp.dot(lhs, data, preferred_element_type=F32)
        aligned = aligned[0:64] + aligned[64:128] + aligned[128:192]
        for rg in range(8):
            value = aligned[8 * rg:8 * rg + 8] * scale + offset
            for h in range(2):
                for q in range(lane_tiles):
                    t = q * CHUNKS + 2 * rg + h
                    piece[m, :, 128 * t:128 * (t + 1)] = value[4 * h:4 * h + 3, 128 * q:128 * (q + 1)]
        target = out.at[:, columns(lax.rem(x + m, 4) * 2 + core)]
        placed.append(pltpu.make_async_remote_copy(
            piece.at[m], target, send4.at[m], recv4.at[m],
            device_id=(frame_at(FRAMES - 2), block), device_id_type=MESH))
        placed[-1].start()
        own.append(pltpu.make_async_copy(piece.at[m], target, out_sem.at[m]))
        own[-1].start()

    finish(0, z[0:coord_rows, :])
    for m in range(1, 4):
        own[m].wait()
        for copy in rest[m - 1]:
            copy.wait_recv()
        finish(m, others[m - 1])

    back = FRAMES / jnp.sqrt(variance1)
    entries = [m * back for m in m2] + [shift * back]
    line = jnp.zeros((8, 128), F32)
    for j in range(4):
        value = jnp.sum(jnp.where(lane == frame, entries[j], 0.0), axis=1, keepdims=True)
        line = jnp.where((lane == 4 * sub + j) & (sub < 3), value, line)
    maps[...] = jnp.sum(line, axis=0, keepdims=True)[:, 0:12]

    for copy in own[4:]:
        copy.wait()
    for copy in placed:
        copy.wait_recv()
    for copy in exchange + sends + rest[0] + rest[1] + rest[2] + placed:
        copy.wait_send()


def solution(mesh):
    blocks = mesh.shape["atoms"]
    ny = min(8, blocks)
    nz = blocks // ny

    def per_device(coords, start):
        atoms = start.shape[1]
        share = atoms // FRAMES
        width = share // CHUNKS
        dma = pltpu.SemaphoreType.DMA
        return pl.pallas_call(
            functools.partial(kernel, ny, nz),
            out_shape=(
                jax.ShapeDtypeStruct((3, atoms), F32),
                jax.ShapeDtypeStruct((1, 12), F32),
            ),
            in_specs=[pl.BlockSpec(memory_space=pltpu.HBM)] * 2,
            out_specs=(
                pl.BlockSpec(memory_space=pl.ANY),
                pl.BlockSpec(memory_space=pltpu.VMEM),
            ),
            scratch_shapes=[
                pltpu.VMEM((FRAMES, 3, share), BF16),
                pltpu.VMEM((3, share), F32),
                pltpu.VMEM((4 * (share // 128), 128), F32),
                pltpu.VMEM((FRAMES, 3 * CHUNKS, width), BF16),
                pltpu.VMEM((32 * CHUNKS, width), BF16),
                pltpu.VMEM((3, 3 * FRAMES * CHUNKS, width), BF16),
                pltpu.VMEM((3, 8, 8, 128), F32),
                pltpu.VMEM((4, 3, share), F32),
                dma((FRAMES + 1,)),
                dma((FRAMES - 1,)),
                dma((FRAMES - 1,)),
                dma((3, 8)),
                dma((3, 8)),
                dma((3, FRAMES - 1)),
                dma((3, FRAMES - 1)),
                dma((4,)),
                dma((4,)),
                dma((4,)),
                dma((4,)),
            ],
            compiler_params=pltpu.CompilerParams(
                collective_id=0, has_side_effects=True, vmem_limit_bytes=60 * 1024 * 1024
            ),
        )(coords, start)

    return jax.shard_map(
        per_device,
        mesh=mesh,
        in_specs=(P("frames", None, "atoms"), P(None, "atoms")),
        out_specs=(P(None, "atoms"), P("frames", None)),
        check_vma=False,
    )
```

```python
import functools

import jax
import jax.numpy as jnp
from jax import lax
from jax.experimental import pallas as pl
from jax.experimental.pallas import tpu as pltpu
from jax.sharding import PartitionSpec as P

MESH = pl.DeviceIdType.MESH
F32, BF16 = jnp.float32, jnp.bfloat16
eps = 1e-06
FRAMES = 8
CHUNKS = 16
OFFSETS = ((2, 0), (2, 1), (1, 0), (1, 1), (3, 0), (3, 1), (0, 1), (0, 0))


def iota(shape, dim):
    return lax.broadcasted_iota(jnp.int32, shape, dim)


def split3(value):
    high = value.astype(BF16)
    rest = value - high.astype(F32)
    middle = rest.astype(BF16)
    low = (rest - middle.astype(F32)).astype(BF16)
    return high, middle, low


def kernel(ny, nz, coords, start, out, maps, xin, rin, tmp, packed, z, others, far, sums,
           in_sem, send1, recv1, send2, recv2, send3, recv3, send4, recv4, own_sem):
    frame = lax.axis_index("frames")
    block = lax.axis_index("atoms")
    x, core = frame // 2, frame % 2
    row, col = block // ny, block % ny
    share = rin.shape[1]
    tiles = share // 128
    width = share // CHUNKS
    lane_tiles = width // 128
    atom_count = float(share * FRAMES * ny * nz)

    def frame_at(k):
        dx, dc = OFFSETS[k]
        return lax.rem(x + dx, 4) * 2 + lax.rem(core + dc, 2)

    def columns(index):
        return pl.ds(pl.multiple_of(index * share, share), share)

    barrier = pltpu.get_barrier_semaphore()
    for k in range(FRAMES - 1):
        pl.semaphore_signal(barrier, inc=1, device_id=(frame_at(k), block), device_id_type=MESH)
    for d in range(1, ny):
        pl.semaphore_signal(
            barrier, inc=1, device_id=(frame, row * ny + lax.rem(col + d, ny)), device_id_type=MESH)
    for d in range(1, nz):
        pl.semaphore_signal(
            barrier, inc=1, device_id=(frame, lax.rem(row + d, nz) * ny + col), device_id_type=MESH)

    loads = []
    for k in range(FRAMES):
        loads.append(pltpu.make_async_copy(
            coords.at[0, :, columns(frame_at(k))], xin.at[k], in_sem.at[k]))
        loads[-1].start()
    load_start = pltpu.make_async_copy(start.at[:, columns(frame)], rin, in_sem.at[FRAMES])
    load_start.start()

    def spread_tiles(load):
        for t in range(tiles):
            tmp[4 * t:4 * t + 3, :] = load(t)

    def dense(j, q):
        return tmp[pl.ds(j + 4 * CHUNKS * q, CHUNKS, stride=4), :]

    own_rows = pl.ds(pl.multiple_of(frame * 3 * CHUNKS, 3 * CHUNKS), 3 * CHUNKS)
    exchange = []
    for k in range(FRAMES):
        loads[k].wait()
        spread_tiles(lambda t: xin[k, :, 128 * t:128 * (t + 1)].astype(F32))
        for j in range(3):
            for q in range(lane_tiles):
                packed[frame_at(k), CHUNKS * j:CHUNKS * (j + 1), 128 * q:128 * (q + 1)] = dense(j, q).astype(BF16)
        if k == 0:
            pl.semaphore_wait(barrier, FRAMES - 1 + ny - 1 + nz - 1)
        if k < FRAMES - 1:
            exchange.append(pltpu.make_async_remote_copy(
                packed.at[frame_at(k)], z.at[own_rows], send1.at[k], recv1.at[k],
                device_id=(frame_at(k), block), device_id_type=MESH))
            exchange[-1].start()
    own = [pltpu.make_async_copy(packed.at[frame], z.at[own_rows], own_sem.at[0])]
    for m in range(1, 4):
        own.append(pltpu.make_async_copy(
            packed.at[lax.rem(x + m, 4) * 2 + core], others.at[m - 1, own_rows], own_sem.at[m]))
    for copy in own:
        copy.start()

    coord_rows = 3 * FRAMES * CHUNKS
    z[coord_rows:coord_rows + CHUNKS, :] = jnp.ones((CHUNKS, width), BF16)
    z[coord_rows + 7 * CHUNKS:coord_rows + 8 * CHUNKS, :] = jnp.zeros((CHUNKS, width), BF16)
    load_start.wait()
    spread_tiles(lambda t: rin[:, 128 * t:128 * (t + 1)])
    for j in range(3):
        for q in range(lane_tiles):
            value = dense(j, q)
            high = value.astype(BF16)
            low = (value - high.astype(F32)).astype(BF16)
            at = coord_rows + CHUNKS * (1 + j)
            z[at:at + CHUNKS, 128 * q:128 * (q + 1)] = high
            z[at + 3 * CHUNKS:at + 4 * CHUNKS, 128 * q:128 * (q + 1)] = low

    total_rows = coord_rows + 8 * CHUNKS
    group = iota((total_rows, 128), 0) >> 4
    place = jnp.where(group == 3 * FRAMES, group, (group % 3) * FRAMES + group // 3)
    collect = jnp.where(
        (place == iota((total_rows, 128), 1)) & (group <= 3 * FRAMES), 1.0, 0.0).astype(BF16)
    same_chunk = iota((CHUNKS, total_rows), 0) == (iota((CHUNKS, total_rows), 1) & (CHUNKS - 1))
    sub = iota((8, 128), 0)
    lane = iota((8, 128), 1)

    own[0].wait()
    for k in range(FRAMES - 1):
        exchange[k].wait_recv()

    groups = 3 * FRAMES + 7
    gram = lax.dot_general(
        z[0:groups * CHUNKS, :], z[...], (((1,), (1,)), ((), ())), preferred_element_type=F32)
    gram = jnp.where(same_chunk[None], gram.reshape(groups, CHUNKS, total_rows), 0.0)
    gram = (gram[:, :8] + gram[:, 8:]).reshape(groups * 8, total_rows)
    gram = sum(jnp.dot(part, collect, preferred_element_type=F32) for part in split3(gram))
    gram = gram.reshape(groups, 8, 128)

    def moment_row(g):
        return jnp.sum(gram[g], axis=0, keepdims=True)

    moments = jnp.zeros((8, 128), F32)
    for j in range(3):
        rows_j = jnp.zeros((8, 128), F32)
        for f in range(FRAMES):
            rows_j = jnp.where(sub == f, moment_row(3 * f + j), rows_j)
        moments = moments + (pltpu.roll(rows_j, 32 * j, 1) if j else rows_j)
    rows_3 = jnp.zeros((8, 128), F32)
    for a in range(3):
        rows_3 = jnp.where(
            (sub & 3) == a, moment_row(3 * FRAMES + 1 + a) + moment_row(3 * FRAMES + 4 + a), rows_3)
    rows_3 = jnp.where((sub & 3) == 3, moment_row(3 * FRAMES), rows_3)
    moments = moments + pltpu.roll(rows_3, 96, 1)

    sends = []
    def far_first(size):
        return sorted(range(1, size), key=lambda d: -min(d, size - d))

    stages = (
        (FRAMES, frame, range(FRAMES - 1), lambda d: (frame_at(d), block)),
        (ny, col, far_first(ny), lambda d: (frame, row * ny + lax.rem(col + d, ny))),
        (nz, row, far_first(nz), lambda d: (frame, lax.rem(row + d, nz) * ny + col)),
    )
    sibling = (frame_at(FRAMES - 2), block)
    passed = [pltpu.make_async_remote_copy(
        z.at[0:coord_rows], far.at[0], send4.at[0], recv4.at[0], device_id=sibling, device_id_type=MESH)]
    last = 2 if nz > 1 else 1
    rest = []
    for stage, (size, me, order, partner) in enumerate(stages):
        if size == 1:
            continue
        sums[stage, me] = moments
        copies = []
        for d in order:
            copies.append(pltpu.make_async_remote_copy(
                sums.at[stage, me], sums.at[stage, me], send2.at[stage, d], recv2.at[stage, d],
                device_id=partner(d), device_id_type=MESH))
            copies[-1].start()
        if stage == 0:
            passed[0].start()
            for m in range(1, 4):
                rest.append([])
                for k in range(FRAMES - 1):
                    to = frame_at(k)
                    rest[-1].append(pltpu.make_async_remote_copy(
                        packed.at[lax.rem(to // 2 + m, 4) * 2 + to % 2], others.at[m - 1, own_rows],
                        send3.at[m - 1, k], recv3.at[m - 1, k], device_id=(to, block), device_id_type=MESH))
                    rest[-1][-1].start()
        if stage == last:
            for m in range(1, 4):
                own[m].wait()
                for copy in rest[m - 1]:
                    copy.wait_recv()
                passed.append(pltpu.make_async_remote_copy(
                    others.at[m - 1], far.at[m], send4.at[m], recv4.at[m], device_id=sibling, device_id_type=MESH))
                passed[-1].start()
        for copy in copies:
            copy.wait_recv()
        sends += copies
        moments = sums[stage, 0]
        for s in range(1, size):
            moments = moments + sums[stage, s]

    inside = lane < 3 * FRAMES + 1
    r = [jnp.where(inside, moments if j == 0 else pltpu.roll(moments, 128 - 32 * j, 1), 0.0) for j in range(4)]
    mean_row = r[3][3:4, :] * (1.0 / atom_count)
    at = 3 * FRAMES
    centred = [v - v[:, at:at + 1] * mean_row for v in r]

    def block_of(value, i):
        return value if i == 0 else pltpu.roll(value, 128 - FRAMES * i, 1)

    diagonal = (lane & (FRAMES - 1)) == sub
    gd = [jnp.broadcast_to(jnp.sum(jnp.where(diagonal, centred[j], 0.0), axis=0, keepdims=True), (8, 128))
          for j in range(3)]
    first = lane < FRAMES
    one = jnp.ones((8, 128), F32)
    g00, g11, g22 = (jnp.where(first, block_of(gd[j], j), one) for j in range(3))
    g01, g02, g12 = (jnp.where(first, v, 0.0) for v in (block_of(gd[0], 1), block_of(gd[0], 2), block_of(gd[1], 2)))
    i0 = 1.0 / g00
    l10, l20 = g01 * i0, g02 * i0
    i1 = 1.0 / (g11 - l10 * g01)
    t12 = g12 - l20 * g01
    l21 = t12 * i1
    i2 = 1.0 / (g22 - l20 * g02 - l21 * t12)

    def solve(c):
        y0 = c[0]
        y1 = c[1] - l10 * y0
        y2 = c[2] - l20 * y0 - l21 * y1
        x2 = y2 * i2
        x1 = y1 * i1 - l21 * x2
        x0 = y0 * i0 - l10 * x1 - l20 * x2
        return [x0, x1, x2]

    def blocks(value):
        return [jnp.where(first, block_of(value, i), 0.0) for i in range(3)]

    def cross(maps_t):
        parts = []
        for j in range(3):
            total = None
            for f in range(FRAMES):
                term = maps_t[j][:, f:f + 1] * centred[j][f:f + 1, :]
                total = term if total is None else total + term
            parts.append(total)
        return blocks(parts[0] + parts[1] + parts[2])

    used = (sub < 3) & first

    def square_mean(maps_t, crosses):
        value = sum(m * c for m, c in zip(maps_t, crosses))
        value = jnp.sum(jnp.where(used, value, 0.0), axis=0, keepdims=True)
        return jnp.sum(value, axis=1, keepdims=True) * (1.0 / atom_count)

    share_of = 1.0 / FRAMES
    m1 = [v * share_of for v in solve(blocks(centred[3]))]
    c1 = cross(m1)
    m2 = [v * share_of for v in solve(c1)]
    c2 = cross(m2)
    variance1 = square_mean(m1, c1) + eps
    variance2 = square_mean(m2, c2) + eps * variance1
    scale = 1.0 / jnp.sqrt(variance2)

    mean_blocks = blocks(jnp.broadcast_to(mean_row, (8, 128)))
    shift = -sum(m * v for m, v in zip(m2, mean_blocks))
    offset = jnp.sum(shift, axis=1, keepdims=True) * scale

    joined = m2[0] + pltpu.roll(m2[1], FRAMES, 1) + pltpu.roll(m2[2], 2 * FRAMES, 1)
    stacked = jnp.concatenate([v.astype(F32) for v in split3(joined)], axis=0).astype(BF16)
    source = iota((128, coord_rows), 1) >> 4
    expand = jnp.where((source % 3) * FRAMES + source // 3 == iota((128, coord_rows), 0), 1.0, 0.0).astype(BF16)
    wide = jnp.dot(stacked, expand, preferred_element_type=F32)
    chunk = iota((8, coord_rows), 1) & (CHUNKS - 1)
    half = iota((8, coord_rows), 0) >> 2
    lhs = jnp.concatenate(
        [jnp.where(chunk == half + 2 * rg, wide[8 * s:8 * s + 8], 0.0) for s in range(3) for rg in range(8)],
        axis=0).astype(BF16)
    def finish(m, side, data):
        base = pl.multiple_of((lax.rem(x + m, 4) * 2 + side) * share, share)
        aligned = jnp.dot(lhs, data, preferred_element_type=F32)
        aligned = aligned[0:64] + aligned[64:128] + aligned[128:192]
        for rg in range(8):
            value = aligned[8 * rg:8 * rg + 8] * scale + offset
            for h in range(2):
                for q in range(lane_tiles):
                    t = q * CHUNKS + 2 * rg + h
                    out[:, pl.ds(pl.multiple_of(base + 128 * t, 128), 128)] = (
                        value[4 * h:4 * h + 3, 128 * q:128 * (q + 1)])

    finish(0, core, z[0:coord_rows, :])
    for m in range(1, 4):
        finish(m, core, others[m - 1])
    for m in range(4):
        passed[m].wait_recv()
        finish(m, 1 - core, far[m])

    back = FRAMES / jnp.sqrt(variance1)
    entries = [m * back for m in m2] + [shift * back]
    line = jnp.zeros((8, 128), F32)
    for j in range(4):
        value = jnp.sum(jnp.where(lane == frame, entries[j], 0.0), axis=1, keepdims=True)
        line = jnp.where((lane == 4 * sub + j) & (sub < 3), value, line)
    maps[...] = jnp.sum(line, axis=0, keepdims=True)[:, 0:12]

    for copy in exchange + sends + rest[0] + rest[1] + rest[2] + passed:
        copy.wait_send()


def solution(mesh):
    blocks = mesh.shape["atoms"]
    ny = min(8, blocks)
    nz = blocks // ny

    def hbm(value):
        return pltpu.with_memory_space_constraint(value, pltpu.HBM)

    def per_device(coords, start):
        atoms = start.shape[1]
        share = atoms // FRAMES
        width = share // CHUNKS
        dma = pltpu.SemaphoreType.DMA
        return pl.pallas_call(
            functools.partial(kernel, ny, nz),
            out_shape=(
                jax.ShapeDtypeStruct((3, atoms), F32),
                jax.ShapeDtypeStruct((1, 12), F32),
            ),
            in_specs=[pl.BlockSpec(memory_space=pltpu.HBM)] * 2,
            out_specs=(
                pl.BlockSpec(memory_space=pltpu.VMEM),
                pl.BlockSpec(memory_space=pltpu.VMEM),
            ),
            scratch_shapes=[
                pltpu.VMEM((FRAMES, 3, share), BF16),
                pltpu.VMEM((3, share), F32),
                pltpu.VMEM((4 * (share // 128), 128), F32),
                pltpu.VMEM((FRAMES, 3 * CHUNKS, width), BF16),
                pltpu.VMEM((32 * CHUNKS, width), BF16),
                pltpu.VMEM((3, 3 * FRAMES * CHUNKS, width), BF16),
                pltpu.VMEM((4, 3 * FRAMES * CHUNKS, width), BF16),
                pltpu.VMEM((3, 8, 8, 128), F32),
                dma((FRAMES + 1,)),
                dma((FRAMES - 1,)),
                dma((FRAMES - 1,)),
                dma((3, 8)),
                dma((3, 8)),
                dma((3, FRAMES - 1)),
                dma((3, FRAMES - 1)),
                dma((4,)),
                dma((4,)),
                dma((4,)),
            ],
            compiler_params=pltpu.CompilerParams(
                collective_id=0, has_side_effects=True, vmem_limit_bytes=40 * 1024 * 1024
            ),
        )(hbm(coords), hbm(start))

    return jax.shard_map(
        per_device,
        mesh=mesh,
        in_specs=(P("frames", None, "atoms"), P(None, "atoms")),
        out_specs=(P(None, "atoms"), P("frames", None)),
        check_vma=False,
    )
```

```python
import functools

import jax
import jax.numpy as jnp
from jax import lax
from jax.experimental import pallas as pl
from jax.experimental.pallas import tpu as pltpu
from jax.sharding import PartitionSpec as P

MESH = pl.DeviceIdType.MESH
F32, BF16 = jnp.float32, jnp.bfloat16
eps = 1e-06
FRAMES = 8
CHUNKS = 16
OFFSETS = ((2, 0), (1, 0), (3, 0), (2, 1), (1, 1), (3, 1), (0, 1), (0, 0))


def iota(shape, dim):
    return lax.broadcasted_iota(jnp.int32, shape, dim)


def split3(value):
    high = value.astype(BF16)
    rest = value - high.astype(F32)
    middle = rest.astype(BF16)
    low = (rest - middle.astype(F32)).astype(BF16)
    return high, middle, low


def kernel(ny, nz, coords, start, out, maps, xin, rin, tmp, packed, z, folded, others, far, sums,
           in_sem, send1, recv1, send2, recv2, send3, recv3, send4, recv4, own_sem):
    frame = lax.axis_index("frames")
    block = lax.axis_index("atoms")
    x, core = frame // 2, frame % 2
    row, col = block // ny, block % ny
    share = rin.shape[1]
    tiles = share // 128
    width = share // CHUNKS
    lane_tiles = width // 128
    atom_count = float(share * FRAMES * ny * nz)

    def frame_at(k):
        dx, dc = OFFSETS[k]
        return lax.rem(x + dx + core * (4 - 2 * dx), 4) * 2 + lax.rem(core + dc, 2)

    def columns(index):
        return pl.ds(pl.multiple_of(index * share, share), share)

    def far_first(size):
        return sorted(range(1, size), key=lambda d: -min(d, size - d))

    barrier = pltpu.get_barrier_semaphore()
    for d in far_first(nz):
        pl.semaphore_signal(
            barrier, inc=1, device_id=(frame, lax.rem(row + d, nz) * ny + col), device_id_type=MESH)
    for d in far_first(ny):
        pl.semaphore_signal(
            barrier, inc=1, device_id=(frame, row * ny + lax.rem(col + d, ny)), device_id_type=MESH)
    for k in range(FRAMES - 1):
        pl.semaphore_signal(barrier, inc=1, device_id=(frame_at(k), block), device_id_type=MESH)

    loads = []
    for k in range(FRAMES):
        loads.append(pltpu.make_async_copy(
            coords.at[0, :, columns(frame_at(k))], xin.at[k], in_sem.at[k]))
        loads[-1].start()
    load_start = pltpu.make_async_copy(start.at[:, columns(frame)], rin, in_sem.at[FRAMES])
    load_start.start()

    def spread_tiles(load):
        for t in range(tiles):
            tmp[4 * t:4 * t + 3, :] = load(t)

    def dense(j, q):
        return tmp[pl.ds(j + 4 * CHUNKS * q, CHUNKS, stride=4), :]

    own_rows = pl.ds(pl.multiple_of(frame * 3 * CHUNKS, 3 * CHUNKS), 3 * CHUNKS)
    exchange = []
    for k in range(FRAMES):
        loads[k].wait()
        spread_tiles(lambda t: xin[k, :, 128 * t:128 * (t + 1)].astype(F32))
        for j in range(3):
            for q in range(lane_tiles):
                packed[frame_at(k), CHUNKS * j:CHUNKS * (j + 1), 128 * q:128 * (q + 1)] = dense(j, q).astype(BF16)
        if k == 0:
            pl.semaphore_wait(barrier, FRAMES - 1 + ny - 1 + nz - 1)
        if k < FRAMES - 1:
            exchange.append(pltpu.make_async_remote_copy(
                packed.at[frame_at(k)], z.at[own_rows], send1.at[k], recv1.at[k],
                device_id=(frame_at(k), block), device_id_type=MESH))
            exchange[-1].start()
    own = [pltpu.make_async_copy(packed.at[frame], z.at[own_rows], own_sem.at[0])]
    for m in range(1, 4):
        own.append(pltpu.make_async_copy(
            packed.at[lax.rem(x + m, 4) * 2 + core], others.at[m - 1, own_rows], own_sem.at[m]))
    for copy in own:
        copy.start()

    coord_rows = 3 * FRAMES * CHUNKS
    load_start.wait()
    spread_tiles(lambda t: rin[:, 128 * t:128 * (t + 1)])
    for q in range(lane_tiles):
        values = [dense(j, q) for j in range(3)]
        highs = [value.astype(BF16).astype(F32) for value in values]
        lows = [value - high for value, high in zip(values, highs)]
        rows = [jnp.ones((CHUNKS, 128), F32)] + highs + lows + [jnp.zeros((CHUNKS, 128), F32)]
        for n in range(4):
            for h in range(2):
                pair = jnp.concatenate([v[8 * h:8 * h + 8] for v in rows[2 * n:2 * n + 2]], axis=0)
                at = coord_rows // 2 + CHUNKS * n
                folded[at:at + CHUNKS, h * width + 128 * q:h * width + 128 * (q + 1)] = pair.astype(BF16)

    groups = 3 * FRAMES + 8
    total_rows = groups * 8
    group = iota((total_rows, 128), 0) >> 3
    place = jnp.where(group == 3 * FRAMES, group, (group % 3) * FRAMES + group // 3)
    collect = jnp.where(
        (place == iota((total_rows, 128), 1)) & (group <= 3 * FRAMES), 1.0, 0.0).astype(BF16)
    same_chunk = iota((8, total_rows), 0) == (iota((8, total_rows), 1) & 7)
    sub = iota((8, 128), 0)
    lane = iota((8, 128), 1)

    own[0].wait()
    for k in range(FRAMES - 1):
        exchange[k].wait_recv()

    for n in range(3 * FRAMES // 2):
        pair = [z[CHUNKS * g:CHUNKS * (g + 1), :].astype(F32) for g in (2 * n, 2 * n + 1)]
        for h in range(2):
            folded[CHUNKS * n:CHUNKS * (n + 1), h * width:(h + 1) * width] = jnp.concatenate(
                [v[8 * h:8 * h + 8] for v in pair], axis=0).astype(BF16)
    gram = lax.dot_general(
        folded[...], folded[...], (((1,), (1,)), ((), ())), preferred_element_type=F32)
    gram = jnp.where(same_chunk[None], gram.reshape(groups, 8, total_rows), 0.0).reshape(total_rows, total_rows)
    gram = sum(jnp.dot(part, collect, preferred_element_type=F32) for part in split3(gram))
    gram = gram.reshape(groups, 8, 128)

    def moment_row(g):
        return jnp.sum(gram[g], axis=0, keepdims=True)

    moments = jnp.zeros((8, 128), F32)
    for j in range(3):
        rows_j = jnp.zeros((8, 128), F32)
        for f in range(FRAMES):
            rows_j = jnp.where(sub == f, moment_row(3 * f + j), rows_j)
        moments = moments + (pltpu.roll(rows_j, 32 * j, 1) if j else rows_j)
    rows_3 = jnp.zeros((8, 128), F32)
    for a in range(3):
        rows_3 = jnp.where(
            (sub & 3) == a, moment_row(3 * FRAMES + 1 + a) + moment_row(3 * FRAMES + 4 + a), rows_3)
    rows_3 = jnp.where((sub & 3) == 3, moment_row(3 * FRAMES), rows_3)
    moments = moments + pltpu.roll(rows_3, 96, 1)

    sends = []
    stages = (
        (FRAMES, frame, range(FRAMES - 1), lambda d: (frame_at(d), block)),
        (ny, col, far_first(ny), lambda d: (frame, row * ny + lax.rem(col + d, ny))),
        (nz, row, far_first(nz), lambda d: (frame, lax.rem(row + d, nz) * ny + col)),
    )
    sibling = (frame_at(FRAMES - 2), block)
    passed = [pltpu.make_async_remote_copy(
        z, far.at[0], send4.at[0], recv4.at[0], device_id=sibling, device_id_type=MESH)]
    last = 2 if nz > 1 else 1
    rest = []
    for stage, (size, me, order, partner) in enumerate(stages):
        if size == 1:
            continue
        sums[stage, me] = moments
        copies = []
        for d in order:
            copies.append(pltpu.make_async_remote_copy(
                sums.at[stage, me], sums.at[stage, me], send2.at[stage, d], recv2.at[stage, d],
                device_id=partner(d), device_id_type=MESH))
            copies[-1].start()
        if stage == 0:
            passed[0].start()
            for m in range(1, 4):
                rest.append([])
                for k in range(FRAMES - 1):
                    to = frame_at(k)
                    rest[-1].append(pltpu.make_async_remote_copy(
                        packed.at[lax.rem(to // 2 + m, 4) * 2 + to % 2], others.at[m - 1, own_rows],
                        send3.at[m - 1, k], recv3.at[m - 1, k], device_id=(to, block), device_id_type=MESH))
                    rest[-1][-1].start()
        if stage == last:
            for m in range(1, 4):
                own[m].wait()
                for copy in rest[m - 1]:
                    copy.wait_recv()
                passed.append(pltpu.make_async_remote_copy(
                    others.at[m - 1], far.at[m], send4.at[m], recv4.at[m], device_id=sibling, device_id_type=MESH))
                passed[-1].start()
        for copy in copies:
            copy.wait_recv()
        sends += copies
        moments = sums[stage, 0]
        for s in range(1, size):
            moments = moments + sums[stage, s]

    inside = lane < 3 * FRAMES + 1
    r = [jnp.where(inside, moments if j == 0 else pltpu.roll(moments, 128 - 32 * j, 1), 0.0) for j in range(4)]
    mean_row = r[3][3:4, :] * (1.0 / atom_count)
    at = 3 * FRAMES
    centred = [v - v[:, at:at + 1] * mean_row for v in r]

    def block_of(value, i):
        return value if i == 0 else pltpu.roll(value, 128 - FRAMES * i, 1)

    diagonal = (lane & (FRAMES - 1)) == sub
    gd = [jnp.broadcast_to(jnp.sum(jnp.where(diagonal, centred[j], 0.0), axis=0, keepdims=True), (8, 128))
          for j in range(3)]
    first = lane < FRAMES
    one = jnp.ones((8, 128), F32)
    g00, g11, g22 = (jnp.where(first, block_of(gd[j], j), one) for j in range(3))
    g01, g02, g12 = (jnp.where(first, v, 0.0) for v in (block_of(gd[0], 1), block_of(gd[0], 2), block_of(gd[1], 2)))
    i0 = 1.0 / g00
    l10, l20 = g01 * i0, g02 * i0
    i1 = 1.0 / (g11 - l10 * g01)
    t12 = g12 - l20 * g01
    l21 = t12 * i1
    i2 = 1.0 / (g22 - l20 * g02 - l21 * t12)

    def solve(c):
        y0 = c[0]
        y1 = c[1] - l10 * y0
        y2 = c[2] - l20 * y0 - l21 * y1
        x2 = y2 * i2
        x1 = y1 * i1 - l21 * x2
        x0 = y0 * i0 - l10 * x1 - l20 * x2
        return [x0, x1, x2]

    def blocks(value):
        return [jnp.where(first, block_of(value, i), 0.0) for i in range(3)]

    def cross(maps_t):
        parts = []
        for j in range(3):
            total = None
            for f in range(FRAMES):
                term = maps_t[j][:, f:f + 1] * centred[j][f:f + 1, :]
                total = term if total is None else total + term
            parts.append(total)
        return blocks(parts[0] + parts[1] + parts[2])

    used = (sub < 3) & first

    def square_mean(maps_t, crosses):
        value = sum(m * c for m, c in zip(maps_t, crosses))
        value = jnp.sum(jnp.where(used, value, 0.0), axis=0, keepdims=True)
        return jnp.sum(value, axis=1, keepdims=True) * (1.0 / atom_count)

    share_of = 1.0 / FRAMES
    m1 = [v * share_of for v in solve(blocks(centred[3]))]
    c1 = cross(m1)
    m2 = [v * share_of for v in solve(c1)]
    c2 = cross(m2)
    variance1 = square_mean(m1, c1) + eps
    variance2 = square_mean(m2, c2) + eps * variance1
    scale = 1.0 / jnp.sqrt(variance2)

    mean_blocks = blocks(jnp.broadcast_to(mean_row, (8, 128)))
    shift = -sum(m * v for m, v in zip(m2, mean_blocks))
    offset = jnp.sum(shift, axis=1, keepdims=True) * scale

    joined = m2[0] + pltpu.roll(m2[1], FRAMES, 1) + pltpu.roll(m2[2], 2 * FRAMES, 1)
    stacked = jnp.concatenate([v.astype(F32) for v in split3(joined)], axis=0).astype(BF16)
    source = iota((128, coord_rows), 1) >> 4
    expand = jnp.where((source % 3) * FRAMES + source // 3 == iota((128, coord_rows), 0), 1.0, 0.0).astype(BF16)
    wide = jnp.dot(stacked, expand, preferred_element_type=F32)
    chunk = iota((8, coord_rows), 1) & (CHUNKS - 1)
    half = iota((8, coord_rows), 0) >> 2
    lhs = jnp.concatenate(
        [jnp.where(chunk == half + 2 * rg, wide[8 * s:8 * s + 8], 0.0) for s in range(3) for rg in range(8)],
        axis=0).astype(BF16)
    def finish(m, side, data):
        base = pl.multiple_of((lax.rem(x + m, 4) * 2 + side) * share, share)
        aligned = jnp.dot(lhs, data, preferred_element_type=F32)
        aligned = aligned[0:64] + aligned[64:128] + aligned[128:192]
        for rg in range(8):
            value = aligned[8 * rg:8 * rg + 8] * scale + offset
            for h in range(2):
                for q in range(lane_tiles):
                    t = q * CHUNKS + 2 * rg + h
                    out[:, pl.ds(pl.multiple_of(base + 128 * t, 128), 128)] = (
                        value[4 * h:4 * h + 3, 128 * q:128 * (q + 1)])

    finish(0, core, z[...])
    for m in range(1, 4):
        finish(m, core, others[m - 1])
    for m in range(4):
        passed[m].wait_recv()
        finish(m, 1 - core, far[m])

    back = FRAMES / jnp.sqrt(variance1)
    entries = [m * back for m in m2] + [shift * back]
    line = jnp.zeros((8, 128), F32)
    for j in range(4):
        value = jnp.sum(jnp.where(lane == frame, entries[j], 0.0), axis=1, keepdims=True)
        line = jnp.where((lane == 4 * sub + j) & (sub < 3), value, line)
    maps[...] = jnp.sum(line, axis=0, keepdims=True)[:, 0:12]

    for copy in exchange + sends + rest[0] + rest[1] + rest[2] + passed:
        copy.wait_send()


def solution(mesh):
    blocks = mesh.shape["atoms"]
    ny = min(8, blocks)
    nz = blocks // ny

    def hbm(value):
        return pltpu.with_memory_space_constraint(value, pltpu.HBM)

    def per_device(coords, start):
        atoms = start.shape[1]
        share = atoms // FRAMES
        width = share // CHUNKS
        dma = pltpu.SemaphoreType.DMA
        return pl.pallas_call(
            functools.partial(kernel, ny, nz),
            out_shape=(
                jax.ShapeDtypeStruct((3, atoms), F32),
                jax.ShapeDtypeStruct((1, 12), F32),
            ),
            in_specs=[pl.BlockSpec(memory_space=pltpu.HBM)] * 2,
            out_specs=(
                pl.BlockSpec(memory_space=pltpu.VMEM),
                pl.BlockSpec(memory_space=pltpu.VMEM),
            ),
            scratch_shapes=[
                pltpu.VMEM((FRAMES, 3, share), BF16),
                pltpu.VMEM((3, share), F32),
                pltpu.VMEM((4 * (share // 128), 128), F32),
                pltpu.VMEM((FRAMES, 3 * CHUNKS, width), BF16),
                pltpu.VMEM((3 * FRAMES * CHUNKS, width), BF16),
                pltpu.VMEM((32 * 8, 2 * width), BF16),
                pltpu.VMEM((3, 3 * FRAMES * CHUNKS, width), BF16),
                pltpu.VMEM((4, 3 * FRAMES * CHUNKS, width), BF16),
                pltpu.VMEM((3, 8, 8, 128), F32),
                dma((FRAMES + 1,)),
                dma((FRAMES - 1,)),
                dma((FRAMES - 1,)),
                dma((3, 8)),
                dma((3, 8)),
                dma((3, FRAMES - 1)),
                dma((3, FRAMES - 1)),
                dma((4,)),
                dma((4,)),
                dma((4,)),
            ],
            compiler_params=pltpu.CompilerParams(
                collective_id=0, has_side_effects=True, vmem_limit_bytes=40 * 1024 * 1024
            ),
        )(hbm(coords), hbm(start))

    return jax.shard_map(
        per_device,
        mesh=mesh,
        in_specs=(P("frames", None, "atoms"), P(None, "atoms")),
        out_specs=(P(None, "atoms"), P("frames", None)),
        check_vma=False,
    )
```

```python
import functools

import jax
import jax.numpy as jnp
from jax import lax
from jax.experimental import pallas as pl
from jax.experimental.pallas import tpu as pltpu
from jax.sharding import PartitionSpec as P

MESH = pl.DeviceIdType.MESH
F32, BF16 = jnp.float32, jnp.bfloat16
eps = 1e-06
FRAMES = 8
CHUNKS = 16
OFFSETS = ((2, 0), (1, 0), (3, 0), (2, 1), (1, 1), (3, 1), (0, 1), (0, 0))


def iota(shape, dim):
    return lax.broadcasted_iota(jnp.int32, shape, dim)


def split3(value):
    high = value.astype(BF16)
    rest = value - high.astype(F32)
    middle = rest.astype(BF16)
    low = (rest - middle.astype(F32)).astype(BF16)
    return high, middle, low


def kernel(ny, nz, coords, start, out, maps, xin, rin, tmp, packed, z, folded, others, far, sums,
           in_sem, send1, recv1, send2, recv2, send3, recv3, send4, recv4, own_sem, send6, recv6):
    frame = lax.axis_index("frames")
    block = lax.axis_index("atoms")
    x, core = frame // 2, frame % 2
    row, col = block // ny, block % ny
    share = rin.shape[1]
    tiles = share // 128
    width = share // CHUNKS
    lane_tiles = width // 128
    atom_count = float(share * FRAMES * ny * nz)

    def frame_at(k):
        dx, dc = OFFSETS[k]
        return lax.rem(x + dx + core * (4 - 2 * dx), 4) * 2 + lax.rem(core + dc, 2)

    def columns(index):
        return pl.ds(pl.multiple_of(index * share, share), share)

    def far_first(size):
        return sorted(range(1, size), key=lambda d: -min(d, size - d))

    barrier = pltpu.get_barrier_semaphore()
    for d in far_first(nz):
        pl.semaphore_signal(
            barrier, inc=1, device_id=(frame, lax.rem(row + d, nz) * ny + col), device_id_type=MESH)
    for d in far_first(ny):
        pl.semaphore_signal(
            barrier, inc=1, device_id=(frame, row * ny + lax.rem(col + d, ny)), device_id_type=MESH)
    for k in range(FRAMES - 1):
        pl.semaphore_signal(barrier, inc=1, device_id=(frame_at(k), block), device_id_type=MESH)

    loads = []
    for k in range(FRAMES):
        loads.append(pltpu.make_async_copy(
            coords.at[0, :, columns(frame_at(k))], xin.at[k], in_sem.at[k]))
        loads[-1].start()
    load_start = pltpu.make_async_copy(start.at[:, columns(frame)], rin, in_sem.at[FRAMES])
    load_start.start()

    def spread_tiles(load):
        for t in range(tiles):
            tmp[4 * t:4 * t + 3, :] = load(t)

    def dense(j, q):
        return tmp[pl.ds(j + 4 * CHUNKS * q, CHUNKS, stride=4), :]

    def rows_of(index):
        return pl.ds(pl.multiple_of(index * 3 * CHUNKS, 3 * CHUNKS), 3 * CHUNKS)

    own_rows = rows_of(frame)
    exchange = []
    for k in range(FRAMES):
        loads[k].wait()
        spread_tiles(lambda t: xin[k, :, 128 * t:128 * (t + 1)].astype(F32))
        for j in range(3):
            for q in range(lane_tiles):
                packed[frame_at(k), CHUNKS * j:CHUNKS * (j + 1), 128 * q:128 * (q + 1)] = dense(j, q).astype(BF16)
        if k == 0:
            pl.semaphore_wait(barrier, FRAMES - 1 + ny - 1 + nz - 1)
        if k < FRAMES - 1:
            exchange.append(pltpu.make_async_remote_copy(
                packed.at[frame_at(k)], z.at[own_rows], send1.at[k], recv1.at[k],
                device_id=(frame_at(k), block), device_id_type=MESH))
            exchange[-1].start()
    own = [pltpu.make_async_copy(packed.at[frame], z.at[own_rows], own_sem.at[0])]
    for m in range(1, 4):
        own.append(pltpu.make_async_copy(
            packed.at[lax.rem(x + m, 4) * 2 + core], others.at[m - 1, own_rows], own_sem.at[m]))
    for copy in own:
        copy.start()

    coord_rows = 3 * FRAMES * CHUNKS
    load_start.wait()
    spread_tiles(lambda t: rin[:, 128 * t:128 * (t + 1)])
    for q in range(lane_tiles):
        values = [dense(j, q) for j in range(3)]
        highs = [value.astype(BF16).astype(F32) for value in values]
        lows = [value - high for value, high in zip(values, highs)]
        rows = [jnp.ones((CHUNKS, 128), F32)] + highs + lows + [jnp.zeros((CHUNKS, 128), F32)]
        for n in range(4):
            for h in range(2):
                pair = jnp.concatenate([v[8 * h:8 * h + 8] for v in rows[2 * n:2 * n + 2]], axis=0)
                at = coord_rows // 2 + CHUNKS * n
                folded[at:at + CHUNKS, h * width + 128 * q:h * width + 128 * (q + 1)] = pair.astype(BF16)

    groups = 3 * FRAMES + 8
    total_rows = groups * 8
    group = iota((total_rows, 128), 0) >> 3
    place = jnp.where(group == 3 * FRAMES, group, (group % 3) * FRAMES + group // 3)
    collect = jnp.where(
        (place == iota((total_rows, 128), 1)) & (group <= 3 * FRAMES), 1.0, 0.0).astype(BF16)
    same_chunk = iota((8, total_rows), 0) == (iota((8, total_rows), 1) & 7)
    sub = iota((8, 128), 0)
    lane = iota((8, 128), 1)

    own[0].wait()
    for k in range(FRAMES - 1):
        exchange[k].wait_recv()

    for n in range(3 * FRAMES // 2):
        pair = [z[CHUNKS * g:CHUNKS * (g + 1), :].astype(F32) for g in (2 * n, 2 * n + 1)]
        for h in range(2):
            folded[CHUNKS * n:CHUNKS * (n + 1), h * width:(h + 1) * width] = jnp.concatenate(
                [v[8 * h:8 * h + 8] for v in pair], axis=0).astype(BF16)
    gram = lax.dot_general(
        folded[...], folded[...], (((1,), (1,)), ((), ())), preferred_element_type=F32)
    gram = jnp.where(same_chunk[None], gram.reshape(groups, 8, total_rows), 0.0).reshape(total_rows, total_rows)
    gram = sum(jnp.dot(part, collect, preferred_element_type=F32) for part in split3(gram))
    gram = gram.reshape(groups, 8, 128)

    def moment_row(g):
        return jnp.sum(gram[g], axis=0, keepdims=True)

    moments = jnp.zeros((8, 128), F32)
    for j in range(3):
        rows_j = jnp.zeros((8, 128), F32)
        for f in range(FRAMES):
            rows_j = jnp.where(sub == f, moment_row(3 * f + j), rows_j)
        moments = moments + (pltpu.roll(rows_j, 32 * j, 1) if j else rows_j)
    rows_3 = jnp.zeros((8, 128), F32)
    for a in range(3):
        rows_3 = jnp.where(
            (sub & 3) == a, moment_row(3 * FRAMES + 1 + a) + moment_row(3 * FRAMES + 4 + a), rows_3)
    rows_3 = jnp.where((sub & 3) == 3, moment_row(3 * FRAMES), rows_3)
    moments = moments + pltpu.roll(rows_3, 96, 1)

    sends = []
    stages = (
        (FRAMES, frame, range(FRAMES - 1), lambda d: (frame_at(d), block)),
        (ny, col, far_first(ny), lambda d: (frame, row * ny + lax.rem(col + d, ny))),
        (nz, row, far_first(nz), lambda d: (frame, lax.rem(row + d, nz) * ny + col)),
    )
    sibling = (frame_at(FRAMES - 2), block)
    passed = [pltpu.make_async_remote_copy(
        z, far.at[0], send4.at[0], recv4.at[0], device_id=sibling, device_id_type=MESH)]
    last = 2 if nz > 1 else 1
    rest = []
    from_low = rows_of(lax.rem(x + 3, 4) * 2)
    from_high = rows_of(lax.rem(x + 1, 4) * 2 + 1)
    low, high = lax.rem(x + 3, 4) * 2 + core, lax.rem(x + 1, 4) * 2 + core
    relays = []
    for n, (source, m, rows, to) in enumerate((
            (z.at[from_low], 3, from_low, high),
            (z.at[from_high], 1, from_high, low),
            (others.at[1, from_low], 1, from_low, high),
            (others.at[2, from_low], 2, from_low, high),
            (others.at[0, from_high], 2, from_high, low),
            (others.at[1, from_high], 3, from_high, low))):
        relays.append(pltpu.make_async_remote_copy(
            source, others.at[m - 1, rows], send6.at[n], recv6.at[n], device_id=(to, block), device_id_type=MESH))

    def arrived(m, k):
        pltpu.make_async_remote_copy(
            packed.at[0], others.at[m - 1, own_rows], send3.at[m - 1, k], recv3.at[m - 1, k],
            device_id=sibling, device_id_type=MESH).wait_recv()

    low_k, high_k = 1 + 3 * core, 1 + 3 * (1 - core)
    for stage, (size, me, order, partner) in enumerate(stages):
        if size == 1:
            continue
        sums[stage, me] = moments
        copies = []
        for d in order:
            copies.append(pltpu.make_async_remote_copy(
                sums.at[stage, me], sums.at[stage, me], send2.at[stage, d], recv2.at[stage, d],
                device_id=partner(d), device_id_type=MESH))
            copies[-1].start()
        if stage == 0:
            passed[0].start()
            order = [(m, k) for m in (2, 3 - 2 * core) for k in (1, 4)]
            order += [(m, k) for m in (1, 2, 3) for k in (2, 5, 6)]
            order += [(1 + 2 * core, k) for k in (1, 4)]
            for m, k in order:
                to = frame_at(k)
                rest.append(pltpu.make_async_remote_copy(
                    packed.at[lax.rem(to // 2 + m, 4) * 2 + to % 2], others.at[m - 1, own_rows],
                    send3.at[m - 1, k], recv3.at[m - 1, k], device_id=(to, block), device_id_type=MESH))
                rest[-1].start()
            for copy in relays[:2]:
                copy.start()
        if stage == 1:
            for m, k in ((2, low_k), (3, low_k), (1, high_k), (2, high_k)):
                arrived(m, k)
            for copy in relays[2:]:
                copy.start()
        if stage == last:
            arrived(1, low_k)
            arrived(3, high_k)
            for m, via in ((1, (1, 2)), (2, (3, 4)), (3, (0, 5))):
                own[m].wait()
                for k in (2, 5, 6):
                    arrived(m, k)
                for n in via:
                    relays[n].wait_recv()
                passed.append(pltpu.make_async_remote_copy(
                    others.at[m - 1], far.at[m], send4.at[m], recv4.at[m], device_id=sibling, device_id_type=MESH))
                passed[-1].start()
        for copy in copies:
            copy.wait_recv()
        sends += copies
        moments = sums[stage, 0]
        for s in range(1, size):
            moments = moments + sums[stage, s]

    inside = lane < 3 * FRAMES + 1
    r = [jnp.where(inside, moments if j == 0 else pltpu.roll(moments, 128 - 32 * j, 1), 0.0) for j in range(4)]
    mean_row = r[3][3:4, :] * (1.0 / atom_count)
    at = 3 * FRAMES
    centred = [v - v[:, at:at + 1] * mean_row for v in r]

    def block_of(value, i):
        return value if i == 0 else pltpu.roll(value, 128 - FRAMES * i, 1)

    diagonal = (lane & (FRAMES - 1)) == sub
    gd = [jnp.broadcast_to(jnp.sum(jnp.where(diagonal, centred[j], 0.0), axis=0, keepdims=True), (8, 128))
          for j in range(3)]
    first = lane < FRAMES
    one = jnp.ones((8, 128), F32)
    g00, g11, g22 = (jnp.where(first, block_of(gd[j], j), one) for j in range(3))
    g01, g02, g12 = (jnp.where(first, v, 0.0) for v in (block_of(gd[0], 1), block_of(gd[0], 2), block_of(gd[1], 2)))
    i0 = 1.0 / g00
    l10, l20 = g01 * i0, g02 * i0
    i1 = 1.0 / (g11 - l10 * g01)
    t12 = g12 - l20 * g01
    l21 = t12 * i1
    i2 = 1.0 / (g22 - l20 * g02 - l21 * t12)

    def solve(c):
        y0 = c[0]
        y1 = c[1] - l10 * y0
        y2 = c[2] - l20 * y0 - l21 * y1
        x2 = y2 * i2
        x1 = y1 * i1 - l21 * x2
        x0 = y0 * i0 - l10 * x1 - l20 * x2
        return [x0, x1, x2]

    def blocks(value):
        return [jnp.where(first, block_of(value, i), 0.0) for i in range(3)]

    def cross(maps_t):
        parts = []
        for j in range(3):
            total = None
            for f in range(FRAMES):
                term = maps_t[j][:, f:f + 1] * centred[j][f:f + 1, :]
                total = term if total is None else total + term
            parts.append(total)
        return blocks(parts[0] + parts[1] + parts[2])

    used = (sub < 3) & first

    def square_mean(maps_t, crosses):
        value = sum(m * c for m, c in zip(maps_t, crosses))
        value = jnp.sum(jnp.where(used, value, 0.0), axis=0, keepdims=True)
        return jnp.sum(value, axis=1, keepdims=True) * (1.0 / atom_count)

    share_of = 1.0 / FRAMES
    m1 = [v * share_of for v in solve(blocks(centred[3]))]
    c1 = cross(m1)
    m2 = [v * share_of for v in solve(c1)]
    c2 = cross(m2)
    variance1 = square_mean(m1, c1) + eps
    variance2 = square_mean(m2, c2) + eps * variance1
    scale = 1.0 / jnp.sqrt(variance2)

    mean_blocks = blocks(jnp.broadcast_to(mean_row, (8, 128)))
    shift = -sum(m * v for m, v in zip(m2, mean_blocks))
    offset = jnp.sum(shift, axis=1, keepdims=True) * scale

    joined = m2[0] + pltpu.roll(m2[1], FRAMES, 1) + pltpu.roll(m2[2], 2 * FRAMES, 1)
    stacked = jnp.concatenate([v.astype(F32) for v in split3(joined)], axis=0).astype(BF16)
    source = iota((128, coord_rows), 1) >> 4
    expand = jnp.where((source % 3) * FRAMES + source // 3 == iota((128, coord_rows), 0), 1.0, 0.0).astype(BF16)
    wide = jnp.dot(stacked, expand, preferred_element_type=F32)
    chunk = iota((8, coord_rows), 1) & (CHUNKS - 1)
    half = iota((8, coord_rows), 0) >> 2
    lhs = jnp.concatenate(
        [jnp.where(chunk == half + 2 * rg, wide[8 * s:8 * s + 8], 0.0) for s in range(3) for rg in range(8)],
        axis=0).astype(BF16)
    def finish(m, side, data):
        base = pl.multiple_of((lax.rem(x + m, 4) * 2 + side) * share, share)
        aligned = jnp.dot(lhs, data, preferred_element_type=F32)
        aligned = aligned[0:64] + aligned[64:128] + aligned[128:192]
        for rg in range(8):
            value = aligned[8 * rg:8 * rg + 8] * scale + offset
            for h in range(2):
                for q in range(lane_tiles):
                    t = q * CHUNKS + 2 * rg + h
                    out[:, pl.ds(pl.multiple_of(base + 128 * t, 128), 128)] = (
                        value[4 * h:4 * h + 3, 128 * q:128 * (q + 1)])

    finish(0, core, z[...])
    for m in range(1, 4):
        finish(m, core, others[m - 1])
    for m in range(4):
        passed[m].wait_recv()
        finish(m, 1 - core, far[m])

    back = FRAMES / jnp.sqrt(variance1)
    entries = [m * back for m in m2] + [shift * back]
    line = jnp.zeros((8, 128), F32)
    for j in range(4):
        value = jnp.sum(jnp.where(lane == frame, entries[j], 0.0), axis=1, keepdims=True)
        line = jnp.where((lane == 4 * sub + j) & (sub < 3), value, line)
    maps[...] = jnp.sum(line, axis=0, keepdims=True)[:, 0:12]

    for copy in exchange + sends + rest + relays + passed:
        copy.wait_send()


def solution(mesh):
    blocks = mesh.shape["atoms"]
    ny = min(8, blocks)
    nz = blocks // ny

    def hbm(value):
        return pltpu.with_memory_space_constraint(value, pltpu.HBM)

    def per_device(coords, start):
        atoms = start.shape[1]
        share = atoms // FRAMES
        width = share // CHUNKS
        dma = pltpu.SemaphoreType.DMA
        return pl.pallas_call(
            functools.partial(kernel, ny, nz),
            out_shape=(
                jax.ShapeDtypeStruct((3, atoms), F32),
                jax.ShapeDtypeStruct((1, 12), F32),
            ),
            in_specs=[pl.BlockSpec(memory_space=pltpu.HBM)] * 2,
            out_specs=(
                pl.BlockSpec(memory_space=pltpu.VMEM),
                pl.BlockSpec(memory_space=pltpu.VMEM),
            ),
            scratch_shapes=[
                pltpu.VMEM((FRAMES, 3, share), BF16),
                pltpu.VMEM((3, share), F32),
                pltpu.VMEM((4 * (share // 128), 128), F32),
                pltpu.VMEM((FRAMES, 3 * CHUNKS, width), BF16),
                pltpu.VMEM((3 * FRAMES * CHUNKS, width), BF16),
                pltpu.VMEM((32 * 8, 2 * width), BF16),
                pltpu.VMEM((3, 3 * FRAMES * CHUNKS, width), BF16),
                pltpu.VMEM((4, 3 * FRAMES * CHUNKS, width), BF16),
                pltpu.VMEM((3, 8, 8, 128), F32),
                dma((FRAMES + 1,)),
                dma((FRAMES - 1,)),
                dma((FRAMES - 1,)),
                dma((3, 8)),
                dma((3, 8)),
                dma((3, FRAMES - 1)),
                dma((3, FRAMES - 1)),
                dma((4,)),
                dma((4,)),
                dma((4,)),
                dma((6,)),
                dma((6,)),
            ],
            compiler_params=pltpu.CompilerParams(
                collective_id=0, has_side_effects=True, vmem_limit_bytes=40 * 1024 * 1024
            ),
        )(hbm(coords), hbm(start))

    return jax.shard_map(
        per_device,
        mesh=mesh,
        in_specs=(P("frames", None, "atoms"), P(None, "atoms")),
        out_specs=(P(None, "atoms"), P("frames", None)),
        check_vma=False,
    )
```

```python
import functools

import jax
import jax.numpy as jnp
from jax import lax
from jax.experimental import pallas as pl
from jax.experimental.pallas import tpu as pltpu
from jax.sharding import PartitionSpec as P

MESH = pl.DeviceIdType.MESH
F32, BF16 = jnp.float32, jnp.bfloat16
eps = 1e-06
FRAMES = 8
CHUNKS = 16
OFFSETS = ((2, 0), (1, 0), (3, 0), (2, 1), (1, 1), (3, 1), (0, 1), (0, 0))


def iota(shape, dim):
    return lax.broadcasted_iota(jnp.int32, shape, dim)


def split3(value):
    high = value.astype(BF16)
    rest = value - high.astype(F32)
    middle = rest.astype(BF16)
    low = (rest - middle.astype(F32)).astype(BF16)
    return high, middle, low


def kernel(ny, nz, coords, start, out, maps, xin, rin, tmp, packed, z, folded, others, far, sums,
           in_sem, send1, recv1, send2, recv2, send3, recv3, send4, recv4, own_sem, send6, recv6):
    frame = lax.axis_index("frames")
    block = lax.axis_index("atoms")
    x, core = frame // 2, frame % 2
    row, col = block // ny, block % ny
    share = rin.shape[1]
    tiles = share // 128
    width = share // CHUNKS
    lane_tiles = width // 128
    atom_count = float(share * FRAMES * ny * nz)

    def frame_at(k):
        dx, dc = OFFSETS[k]
        return lax.rem(x + dx + core * (4 - 2 * dx), 4) * 2 + lax.rem(core + dc, 2)

    def columns(index):
        return pl.ds(pl.multiple_of(index * share, share), share)

    def far_first(size):
        return sorted(range(1, size), key=lambda d: -min(d, size - d))

    barrier = pltpu.get_barrier_semaphore()
    for d in far_first(nz):
        pl.semaphore_signal(
            barrier, inc=1, device_id=(frame, lax.rem(row + d, nz) * ny + col), device_id_type=MESH)
    for d in far_first(ny):
        pl.semaphore_signal(
            barrier, inc=1, device_id=(frame, row * ny + lax.rem(col + d, ny)), device_id_type=MESH)
    for k in range(FRAMES - 1):
        pl.semaphore_signal(barrier, inc=1, device_id=(frame_at(k), block), device_id_type=MESH)

    loads = []
    for k in range(FRAMES):
        loads.append(pltpu.make_async_copy(
            coords.at[0, :, columns(frame_at(k))], xin.at[k], in_sem.at[k]))
        loads[-1].start()
    load_start = pltpu.make_async_copy(start.at[:, columns(frame)], rin, in_sem.at[FRAMES])
    load_start.start()

    def spread_tiles(load):
        for t in range(tiles):
            tmp[4 * t:4 * t + 3, :] = load(t)

    def dense(j, q):
        return tmp[pl.ds(j + 4 * CHUNKS * q, CHUNKS, stride=4), :]

    def rows_of(index):
        return pl.ds(pl.multiple_of(index * 3 * CHUNKS, 3 * CHUNKS), 3 * CHUNKS)

    own_rows = rows_of(frame)
    exchange = []
    for k in range(FRAMES):
        loads[k].wait()
        spread_tiles(lambda t: xin[k, :, 128 * t:128 * (t + 1)].astype(F32))
        for j in range(3):
            for q in range(lane_tiles):
                packed[frame_at(k), CHUNKS * j:CHUNKS * (j + 1), 128 * q:128 * (q + 1)] = dense(j, q).astype(BF16)
        if k == 0:
            pl.semaphore_wait(barrier, FRAMES - 1 + ny - 1 + nz - 1)
        if k < FRAMES - 1:
            exchange.append(pltpu.make_async_remote_copy(
                packed.at[frame_at(k)], z.at[own_rows], send1.at[k], recv1.at[k],
                device_id=(frame_at(k), block), device_id_type=MESH))
            exchange[-1].start()
    own = [pltpu.make_async_copy(packed.at[frame], z.at[own_rows], own_sem.at[0])]
    for m in range(1, 4):
        own.append(pltpu.make_async_copy(
            packed.at[lax.rem(x + m, 4) * 2 + core], others.at[m - 1, own_rows], own_sem.at[m]))
    for copy in own:
        copy.start()

    coord_rows = 3 * FRAMES * CHUNKS
    load_start.wait()
    spread_tiles(lambda t: rin[:, 128 * t:128 * (t + 1)])
    for q in range(lane_tiles):
        values = [dense(j, q) for j in range(3)]
        highs = [value.astype(BF16).astype(F32) for value in values]
        lows = [value - high for value, high in zip(values, highs)]
        rows = [jnp.ones((CHUNKS, 128), F32)] + highs + lows + [jnp.zeros((CHUNKS, 128), F32)]
        for n in range(4):
            for h in range(2):
                pair = jnp.concatenate([v[8 * h:8 * h + 8] for v in rows[2 * n:2 * n + 2]], axis=0)
                at = coord_rows // 2 + CHUNKS * n
                folded[at:at + CHUNKS, h * width + 128 * q:h * width + 128 * (q + 1)] = pair.astype(BF16)

    groups = 3 * FRAMES + 8
    total_rows = groups * 8
    group = iota((total_rows, 128), 0) >> 3
    place = jnp.where(group == 3 * FRAMES, group, (group % 3) * FRAMES + group // 3)
    collect = jnp.where(
        (place == iota((total_rows, 128), 1)) & (group <= 3 * FRAMES), 1.0, 0.0).astype(BF16)
    same_chunk = iota((8, total_rows), 0) == (iota((8, total_rows), 1) & 7)
    sub = iota((8, 128), 0)
    lane = iota((8, 128), 1)

    own[0].wait()
    for k in range(FRAMES - 1):
        exchange[k].wait_recv()

    for n in range(3 * FRAMES // 2):
        pair = [z[CHUNKS * g:CHUNKS * (g + 1), :].astype(F32) for g in (2 * n, 2 * n + 1)]
        for h in range(2):
            folded[CHUNKS * n:CHUNKS * (n + 1), h * width:(h + 1) * width] = jnp.concatenate(
                [v[8 * h:8 * h + 8] for v in pair], axis=0).astype(BF16)
    gram = lax.dot_general(
        folded[...], folded[...], (((1,), (1,)), ((), ())), preferred_element_type=F32)
    gram = jnp.where(same_chunk[None], gram.reshape(groups, 8, total_rows), 0.0).reshape(total_rows, total_rows)
    gram = jnp.dot(jnp.concatenate(split3(gram), axis=0), collect, preferred_element_type=F32)
    gram = gram[:total_rows] + gram[total_rows:2 * total_rows] + gram[2 * total_rows:]
    gram = gram.reshape(groups, 8, 128)

    def moment_row(g):
        return jnp.sum(gram[g], axis=0, keepdims=True)

    moments = jnp.zeros((8, 128), F32)
    for j in range(3):
        rows_j = jnp.zeros((8, 128), F32)
        for f in range(FRAMES):
            rows_j = jnp.where(sub == f, moment_row(3 * f + j), rows_j)
        moments = moments + (pltpu.roll(rows_j, 32 * j, 1) if j else rows_j)
    rows_3 = jnp.zeros((8, 128), F32)
    for a in range(3):
        rows_3 = jnp.where(
            (sub & 3) == a, moment_row(3 * FRAMES + 1 + a) + moment_row(3 * FRAMES + 4 + a), rows_3)
    rows_3 = jnp.where((sub & 3) == 3, moment_row(3 * FRAMES), rows_3)
    moments = moments + pltpu.roll(rows_3, 96, 1)

    sends = []
    stages = (
        (FRAMES, frame, range(FRAMES - 1), lambda d: (frame_at(d), block)),
        (ny, col, far_first(ny), lambda d: (frame, row * ny + lax.rem(col + d, ny))),
        (nz, row, far_first(nz), lambda d: (frame, lax.rem(row + d, nz) * ny + col)),
    )
    sibling = (frame_at(FRAMES - 2), block)
    passed = [pltpu.make_async_remote_copy(
        z, far.at[0], send4.at[0], recv4.at[0], device_id=sibling, device_id_type=MESH)]
    last = 2 if nz > 1 else 1
    rest = []
    from_low = rows_of(lax.rem(x + 3, 4) * 2)
    from_high = rows_of(lax.rem(x + 1, 4) * 2 + 1)
    low, high = lax.rem(x + 3, 4) * 2 + core, lax.rem(x + 1, 4) * 2 + core
    relays = []
    for n, (source, m, rows, to) in enumerate((
            (z.at[from_low], 3, from_low, high),
            (z.at[from_high], 1, from_high, low),
            (others.at[1, from_low], 1, from_low, high),
            (others.at[2, from_low], 2, from_low, high),
            (others.at[0, from_high], 2, from_high, low),
            (others.at[1, from_high], 3, from_high, low))):
        relays.append(pltpu.make_async_remote_copy(
            source, others.at[m - 1, rows], send6.at[n], recv6.at[n], device_id=(to, block), device_id_type=MESH))

    def arrived(m, k):
        pltpu.make_async_remote_copy(
            packed.at[0], others.at[m - 1, own_rows], send3.at[m - 1, k], recv3.at[m - 1, k],
            device_id=sibling, device_id_type=MESH).wait_recv()

    low_k, high_k = 1 + 3 * core, 1 + 3 * (1 - core)
    for stage, (size, me, order, partner) in enumerate(stages):
        if size == 1:
            continue
        sums[stage, me] = moments
        copies = []
        for d in order:
            copies.append(pltpu.make_async_remote_copy(
                sums.at[stage, me], sums.at[stage, me], send2.at[stage, d], recv2.at[stage, d],
                device_id=partner(d), device_id_type=MESH))
            copies[-1].start()
        if stage == 0:
            passed[0].start()
            order = [(m, k) for m in (2, 3 - 2 * core) for k in (1, 4)]
            order += [(m, k) for m in (1, 2, 3) for k in (2, 5, 6)]
            order += [(1 + 2 * core, k) for k in (1, 4)]
            for m, k in order:
                to = frame_at(k)
                rest.append(pltpu.make_async_remote_copy(
                    packed.at[lax.rem(to // 2 + m, 4) * 2 + to % 2], others.at[m - 1, own_rows],
                    send3.at[m - 1, k], recv3.at[m - 1, k], device_id=(to, block), device_id_type=MESH))
                rest[-1].start()
            for copy in relays[:2]:
                copy.start()
        if stage == 1:
            for m, k in ((2, low_k), (3, low_k), (1, high_k), (2, high_k)):
                arrived(m, k)
            for copy in relays[2:]:
                copy.start()
        if stage == last:
            arrived(1, low_k)
            arrived(3, high_k)
            for m, via in ((1, (1, 2)), (2, (3, 4)), (3, (0, 5))):
                own[m].wait()
                for k in (2, 5, 6):
                    arrived(m, k)
                for n in via:
                    relays[n].wait_recv()
                passed.append(pltpu.make_async_remote_copy(
                    others.at[m - 1], far.at[m], send4.at[m], recv4.at[m], device_id=sibling, device_id_type=MESH))
                passed[-1].start()
        for copy in copies:
            copy.wait_recv()
        sends += copies
        moments = sums[stage, 0]
        for s in range(1, size):
            moments = moments + sums[stage, s]

    inside = lane < 3 * FRAMES + 1
    r = [jnp.where(inside, moments if j == 0 else pltpu.roll(moments, 128 - 32 * j, 1), 0.0) for j in range(4)]
    mean_row = r[3][3:4, :] * (1.0 / atom_count)
    at = 3 * FRAMES
    centred = [v - v[:, at:at + 1] * mean_row for v in r]

    def block_of(value, i):
        return value if i == 0 else pltpu.roll(value, 128 - FRAMES * i, 1)

    diagonal = (lane & (FRAMES - 1)) == sub
    gd = [jnp.broadcast_to(jnp.sum(jnp.where(diagonal, centred[j], 0.0), axis=0, keepdims=True), (8, 128))
          for j in range(3)]
    first = lane < FRAMES
    one = jnp.ones((8, 128), F32)
    g00, g11, g22 = (jnp.where(first, block_of(gd[j], j), one) for j in range(3))
    g01, g02, g12 = (jnp.where(first, v, 0.0) for v in (block_of(gd[0], 1), block_of(gd[0], 2), block_of(gd[1], 2)))
    i0 = 1.0 / g00
    l10, l20 = g01 * i0, g02 * i0
    i1 = 1.0 / (g11 - l10 * g01)
    t12 = g12 - l20 * g01
    l21 = t12 * i1
    i2 = 1.0 / (g22 - l20 * g02 - l21 * t12)

    def solve(c):
        y0 = c[0]
        y1 = c[1] - l10 * y0
        y2 = c[2] - l20 * y0 - l21 * y1
        x2 = y2 * i2
        x1 = y1 * i1 - l21 * x2
        x0 = y0 * i0 - l10 * x1 - l20 * x2
        return [x0, x1, x2]

    def blocks(value):
        return [jnp.where(first, block_of(value, i), 0.0) for i in range(3)]

    def cross(maps_t):
        parts = []
        for j in range(3):
            total = None
            for f in range(FRAMES):
                term = maps_t[j][:, f:f + 1] * centred[j][f:f + 1, :]
                total = term if total is None else total + term
            parts.append(total)
        return blocks(parts[0] + parts[1] + parts[2])

    used = (sub < 3) & first

    def square_mean(maps_t, crosses):
        value = sum(m * c for m, c in zip(maps_t, crosses))
        value = jnp.sum(jnp.where(used, value, 0.0), axis=0, keepdims=True)
        return jnp.sum(value, axis=1, keepdims=True) * (1.0 / atom_count)

    share_of = 1.0 / FRAMES
    m1 = [v * share_of for v in solve(blocks(centred[3]))]
    c1 = cross(m1)
    m2 = [v * share_of for v in solve(c1)]
    c2 = cross(m2)
    variance1 = square_mean(m1, c1) + eps
    variance2 = square_mean(m2, c2) + eps * variance1
    scale = 1.0 / jnp.sqrt(variance2)

    mean_blocks = blocks(jnp.broadcast_to(mean_row, (8, 128)))
    shift = -sum(m * v for m, v in zip(m2, mean_blocks))
    offset = jnp.sum(shift, axis=1, keepdims=True) * scale

    joined = m2[0] + pltpu.roll(m2[1], FRAMES, 1) + pltpu.roll(m2[2], 2 * FRAMES, 1)
    stacked = jnp.concatenate([v.astype(F32) for v in split3(joined)], axis=0).astype(BF16)
    source = iota((128, coord_rows), 1) >> 4
    expand = jnp.where((source % 3) * FRAMES + source // 3 == iota((128, coord_rows), 0), 1.0, 0.0).astype(BF16)
    wide = jnp.dot(stacked, expand, preferred_element_type=F32)
    chunk = iota((8, coord_rows), 1) & (CHUNKS - 1)
    half = iota((8, coord_rows), 0) >> 2
    lhs = jnp.concatenate(
        [jnp.where(chunk == half + 2 * rg, wide[8 * s:8 * s + 8], 0.0) for s in range(3) for rg in range(8)],
        axis=0).astype(BF16)
    def finish(m, side, data):
        base = pl.multiple_of((lax.rem(x + m, 4) * 2 + side) * share, share)
        aligned = jnp.dot(lhs, data, preferred_element_type=F32)
        aligned = aligned[0:64] + aligned[64:128] + aligned[128:192]
        for rg in range(8):
            value = aligned[8 * rg:8 * rg + 8] * scale + offset
            for h in range(2):
                for q in range(lane_tiles):
                    t = q * CHUNKS + 2 * rg + h
                    out[:, pl.ds(pl.multiple_of(base + 128 * t, 128), 128)] = (
                        value[4 * h:4 * h + 3, 128 * q:128 * (q + 1)])

    finish(0, core, z[...])
    for m in range(1, 4):
        finish(m, core, others[m - 1])
    for m in range(4):
        passed[m].wait_recv()
        finish(m, 1 - core, far[m])

    back = FRAMES / jnp.sqrt(variance1)
    entries = [m * back for m in m2] + [shift * back]
    line = jnp.zeros((8, 128), F32)
    for j in range(4):
        value = jnp.sum(jnp.where(lane == frame, entries[j], 0.0), axis=1, keepdims=True)
        line = jnp.where((lane == 4 * sub + j) & (sub < 3), value, line)
    maps[...] = jnp.sum(line, axis=0, keepdims=True)[:, 0:12]

    for copy in exchange + sends + rest + relays + passed:
        copy.wait_send()


def solution(mesh):
    blocks = mesh.shape["atoms"]
    ny = min(8, blocks)
    nz = blocks // ny

    def hbm(value):
        return pltpu.with_memory_space_constraint(value, pltpu.HBM)

    def per_device(coords, start):
        atoms = start.shape[1]
        share = atoms // FRAMES
        width = share // CHUNKS
        dma = pltpu.SemaphoreType.DMA
        return pl.pallas_call(
            functools.partial(kernel, ny, nz),
            out_shape=(
                jax.ShapeDtypeStruct((3, atoms), F32),
                jax.ShapeDtypeStruct((1, 12), F32),
            ),
            in_specs=[pl.BlockSpec(memory_space=pltpu.HBM)] * 2,
            out_specs=(
                pl.BlockSpec(memory_space=pltpu.VMEM),
                pl.BlockSpec(memory_space=pltpu.VMEM),
            ),
            scratch_shapes=[
                pltpu.VMEM((FRAMES, 3, share), BF16),
                pltpu.VMEM((3, share), F32),
                pltpu.VMEM((4 * (share // 128), 128), F32),
                pltpu.VMEM((FRAMES, 3 * CHUNKS, width), BF16),
                pltpu.VMEM((3 * FRAMES * CHUNKS, width), BF16),
                pltpu.VMEM((32 * 8, 2 * width), BF16),
                pltpu.VMEM((3, 3 * FRAMES * CHUNKS, width), BF16),
                pltpu.VMEM((4, 3 * FRAMES * CHUNKS, width), BF16),
                pltpu.VMEM((3, 8, 8, 128), F32),
                dma((FRAMES + 1,)),
                dma((FRAMES - 1,)),
                dma((FRAMES - 1,)),
                dma((3, 8)),
                dma((3, 8)),
                dma((3, FRAMES - 1)),
                dma((3, FRAMES - 1)),
                dma((4,)),
                dma((4,)),
                dma((4,)),
                dma((6,)),
                dma((6,)),
            ],
            compiler_params=pltpu.CompilerParams(
                collective_id=0, has_side_effects=True, vmem_limit_bytes=40 * 1024 * 1024
            ),
        )(hbm(coords), hbm(start))

    return jax.shard_map(
        per_device,
        mesh=mesh,
        in_specs=(P("frames", None, "atoms"), P(None, "atoms")),
        out_specs=(P(None, "atoms"), P("frames", None)),
        check_vma=False,
    )
```

```python
import functools

import jax
import jax.numpy as jnp
from jax import lax
from jax.experimental import pallas as pl
from jax.experimental.pallas import tpu as pltpu
from jax.sharding import PartitionSpec as P

MESH = pl.DeviceIdType.MESH
F32, BF16 = jnp.float32, jnp.bfloat16
eps = 1e-06
FRAMES = 8
CHUNKS = 16
OFFSETS = ((2, 0), (1, 0), (3, 0), (2, 1), (1, 1), (3, 1), (0, 1), (0, 0))


def iota(shape, dim):
    return lax.broadcasted_iota(jnp.int32, shape, dim)


def split3(value):
    high = value.astype(BF16)
    rest = value - high.astype(F32)
    middle = rest.astype(BF16)
    low = (rest - middle.astype(F32)).astype(BF16)
    return high, middle, low


def kernel(ny, nz, coords, start, out, maps, xin, rin, tmp, packed, z, folded, others, far, sums,
           in_sem, send1, recv1, send2, recv2, send3, recv3, send4, recv4, own_sem, send6, recv6):
    frame = lax.axis_index("frames")
    block = lax.axis_index("atoms")
    x, core = frame // 2, frame % 2
    row, col = block // ny, block % ny
    share = rin.shape[1]
    tiles = share // 128
    width = share // CHUNKS
    lane_tiles = width // 128
    atom_count = float(share * FRAMES * ny * nz)

    def frame_at(k):
        dx, dc = OFFSETS[k]
        return lax.rem(x + dx + core * (4 - 2 * dx), 4) * 2 + lax.rem(core + dc, 2)

    def columns(index):
        return pl.ds(pl.multiple_of(index * share, share), share)

    def far_first(size):
        return sorted(range(1, size), key=lambda d: -min(d, size - d))

    barrier = pltpu.get_barrier_semaphore()
    for d in far_first(nz):
        pl.semaphore_signal(
            barrier, inc=1, device_id=(frame, lax.rem(row + d, nz) * ny + col), device_id_type=MESH)
    for d in far_first(ny):
        pl.semaphore_signal(
            barrier, inc=1, device_id=(frame, row * ny + lax.rem(col + d, ny)), device_id_type=MESH)
    for k in range(FRAMES - 1):
        pl.semaphore_signal(barrier, inc=1, device_id=(frame_at(k), block), device_id_type=MESH)

    loads = []
    for k in range(FRAMES):
        loads.append(pltpu.make_async_copy(
            coords.at[0, :, columns(frame_at(k))], xin.at[k], in_sem.at[k]))
        loads[-1].start()
    load_start = pltpu.make_async_copy(start.at[:, columns(frame)], rin, in_sem.at[FRAMES])
    load_start.start()

    def spread_tiles(load):
        for t in range(tiles):
            tmp[4 * t:4 * t + 3, :] = load(t)

    def dense(j, q):
        return tmp[pl.ds(j + 4 * CHUNKS * q, CHUNKS, stride=4), :]

    def rows_of(index):
        return pl.ds(pl.multiple_of(index * 3 * CHUNKS, 3 * CHUNKS), 3 * CHUNKS)

    own_rows = rows_of(frame)
    exchange = []
    for k in range(FRAMES):
        loads[k].wait()
        spread_tiles(lambda t: xin[k, :, 128 * t:128 * (t + 1)].astype(F32))
        for j in range(3):
            for q in range(lane_tiles):
                packed[frame_at(k), CHUNKS * j:CHUNKS * (j + 1), 128 * q:128 * (q + 1)] = dense(j, q).astype(BF16)
        if k == 0:
            pl.semaphore_wait(barrier, FRAMES - 1 + ny - 1 + nz - 1)
        if k < FRAMES - 1:
            exchange.append(pltpu.make_async_remote_copy(
                packed.at[frame_at(k)], z.at[own_rows], send1.at[k], recv1.at[k],
                device_id=(frame_at(k), block), device_id_type=MESH))
            exchange[-1].start()
    own = [pltpu.make_async_copy(packed.at[frame], z.at[own_rows], own_sem.at[0])]
    for m in range(1, 4):
        own.append(pltpu.make_async_copy(
            packed.at[lax.rem(x + m, 4) * 2 + core], others.at[m - 1, own_rows], own_sem.at[m]))
    for copy in own:
        copy.start()

    coord_rows = 3 * FRAMES * CHUNKS
    load_start.wait()
    spread_tiles(lambda t: rin[:, 128 * t:128 * (t + 1)])
    for q in range(lane_tiles):
        values = [dense(j, q) for j in range(3)]
        highs = [value.astype(BF16).astype(F32) for value in values]
        lows = [value - high for value, high in zip(values, highs)]
        rows = [jnp.ones((CHUNKS, 128), F32)] + highs + lows + [jnp.zeros((CHUNKS, 128), F32)]
        for n in range(4):
            for h in range(2):
                pair = jnp.concatenate([v[8 * h:8 * h + 8] for v in rows[2 * n:2 * n + 2]], axis=0)
                at = coord_rows // 2 + CHUNKS * n
                folded[at:at + CHUNKS, h * width + 128 * q:h * width + 128 * (q + 1)] = pair.astype(BF16)

    groups = 3 * FRAMES + 8
    total_rows = groups * 8
    group = iota((total_rows, 128), 0) >> 3
    place = jnp.where(group == 3 * FRAMES, group, (group % 3) * FRAMES + group // 3)
    collect = jnp.where(
        (place == iota((total_rows, 128), 1)) & (group <= 3 * FRAMES), 1.0, 0.0).astype(BF16)
    same_chunk = iota((8, total_rows), 0) == (iota((8, total_rows), 1) & 7)
    sub = iota((8, 128), 0)
    lane = iota((8, 128), 1)

    own[0].wait()
    for k in range(FRAMES - 1):
        exchange[k].wait_recv()

    for n in range(3 * FRAMES // 2):
        pair = [z[CHUNKS * g:CHUNKS * (g + 1), :].astype(F32) for g in (2 * n, 2 * n + 1)]
        for h in range(2):
            folded[CHUNKS * n:CHUNKS * (n + 1), h * width:(h + 1) * width] = jnp.concatenate(
                [v[8 * h:8 * h + 8] for v in pair], axis=0).astype(BF16)
    gram = lax.dot_general(
        folded[...], folded[...], (((1,), (1,)), ((), ())), preferred_element_type=F32)
    gram = jnp.where(same_chunk[None], gram.reshape(groups, 8, total_rows), 0.0).reshape(total_rows, total_rows)
    gram = sum(jnp.dot(part, collect, preferred_element_type=F32) for part in split3(gram))
    gram = gram.reshape(groups, 8, 128)

    def moment_row(g):
        return jnp.sum(gram[g], axis=0, keepdims=True)

    moments = jnp.zeros((8, 128), F32)
    for j in range(3):
        rows_j = jnp.zeros((8, 128), F32)
        for f in range(FRAMES):
            rows_j = jnp.where(sub == f, moment_row(3 * f + j), rows_j)
        moments = moments + (pltpu.roll(rows_j, 32 * j, 1) if j else rows_j)
    rows_3 = jnp.zeros((8, 128), F32)
    for a in range(3):
        rows_3 = jnp.where(
            (sub & 3) == a, moment_row(3 * FRAMES + 1 + a) + moment_row(3 * FRAMES + 4 + a), rows_3)
    rows_3 = jnp.where((sub & 3) == 3, moment_row(3 * FRAMES), rows_3)
    moments = moments + pltpu.roll(rows_3, 96, 1)

    sends = []
    stages = (
        (FRAMES, frame, range(FRAMES - 1), lambda d: (frame_at(d), block)),
        (nz, row, far_first(nz), lambda d: (frame, lax.rem(row + d, nz) * ny + col)),
        (ny, col, far_first(ny), lambda d: (frame, row * ny + lax.rem(col + d, ny))),
    )
    sibling = (frame_at(FRAMES - 2), block)
    passed = [pltpu.make_async_remote_copy(
        z, far.at[0], send4.at[0], recv4.at[0], device_id=sibling, device_id_type=MESH)]
    last = 2 if nz > 1 else 1
    rest = []
    from_low = rows_of(lax.rem(x + 3, 4) * 2)
    from_high = rows_of(lax.rem(x + 1, 4) * 2 + 1)
    low, high = lax.rem(x + 3, 4) * 2 + core, lax.rem(x + 1, 4) * 2 + core
    relays = []
    for n, (source, m, rows, to) in enumerate((
            (z.at[from_low], 3, from_low, high),
            (z.at[from_high], 1, from_high, low),
            (others.at[1, from_low], 1, from_low, high),
            (others.at[2, from_low], 2, from_low, high),
            (others.at[0, from_high], 2, from_high, low),
            (others.at[1, from_high], 3, from_high, low))):
        relays.append(pltpu.make_async_remote_copy(
            source, others.at[m - 1, rows], send6.at[n], recv6.at[n], device_id=(to, block), device_id_type=MESH))

    def arrived(m, k):
        pltpu.make_async_remote_copy(
            packed.at[0], others.at[m - 1, own_rows], send3.at[m - 1, k], recv3.at[m - 1, k],
            device_id=sibling, device_id_type=MESH).wait_recv()

    low_k, high_k = 1 + 3 * core, 1 + 3 * (1 - core)
    for stage, (size, me, order, partner) in enumerate(stages):
        if size == 1:
            continue
        sums[stage, me] = moments
        copies = []
        for d in order:
            copies.append(pltpu.make_async_remote_copy(
                sums.at[stage, me], sums.at[stage, me], send2.at[stage, d], recv2.at[stage, d],
                device_id=partner(d), device_id_type=MESH))
            copies[-1].start()
        if stage == 0:
            passed[0].start()
            order = [(m, k) for m in (2, 3 - 2 * core) for k in (1, 4)]
            order += [(m, k) for m in (1, 2, 3) for k in (2, 5, 6)]
            order += [(1 + 2 * core, k) for k in (1, 4)]
            for m, k in order:
                to = frame_at(k)
                rest.append(pltpu.make_async_remote_copy(
                    packed.at[lax.rem(to // 2 + m, 4) * 2 + to % 2], others.at[m - 1, own_rows],
                    send3.at[m - 1, k], recv3.at[m - 1, k], device_id=(to, block), device_id_type=MESH))
                rest[-1].start()
            for copy in relays[:2]:
                copy.start()
        if stage == 1:
            for m, k in ((2, low_k), (3, low_k), (1, high_k), (2, high_k)):
                arrived(m, k)
            for copy in relays[2:]:
                copy.start()
        if stage == last:
            arrived(1, low_k)
            arrived(3, high_k)
            for m, via in ((1, (1, 2)), (2, (3, 4)), (3, (0, 5))):
                own[m].wait()
                for k in (2, 5, 6):
                    arrived(m, k)
                for n in via:
                    relays[n].wait_recv()
                passed.append(pltpu.make_async_remote_copy(
                    others.at[m - 1], far.at[m], send4.at[m], recv4.at[m], device_id=sibling, device_id_type=MESH))
                passed[-1].start()
        for copy in copies:
            copy.wait_recv()
        sends += copies
        moments = sums[stage, 0]
        for s in range(1, size):
            moments = moments + sums[stage, s]

    inside = lane < 3 * FRAMES + 1
    r = [jnp.where(inside, moments if j == 0 else pltpu.roll(moments, 128 - 32 * j, 1), 0.0) for j in range(4)]
    mean_row = r[3][3:4, :] * (1.0 / atom_count)
    at = 3 * FRAMES
    centred = [v - v[:, at:at + 1] * mean_row for v in r]

    def block_of(value, i):
        return value if i == 0 else pltpu.roll(value, 128 - FRAMES * i, 1)

    diagonal = (lane & (FRAMES - 1)) == sub
    gd = [jnp.broadcast_to(jnp.sum(jnp.where(diagonal, centred[j], 0.0), axis=0, keepdims=True), (8, 128))
          for j in range(3)]
    first = lane < FRAMES
    one = jnp.ones((8, 128), F32)
    g00, g11, g22 = (jnp.where(first, block_of(gd[j], j), one) for j in range(3))
    g01, g02, g12 = (jnp.where(first, v, 0.0) for v in (block_of(gd[0], 1), block_of(gd[0], 2), block_of(gd[1], 2)))
    i0 = 1.0 / g00
    l10, l20 = g01 * i0, g02 * i0
    i1 = 1.0 / (g11 - l10 * g01)
    t12 = g12 - l20 * g01
    l21 = t12 * i1
    i2 = 1.0 / (g22 - l20 * g02 - l21 * t12)

    def solve(c):
        y0 = c[0]
        y1 = c[1] - l10 * y0
        y2 = c[2] - l20 * y0 - l21 * y1
        x2 = y2 * i2
        x1 = y1 * i1 - l21 * x2
        x0 = y0 * i0 - l10 * x1 - l20 * x2
        return [x0, x1, x2]

    def blocks(value):
        return [jnp.where(first, block_of(value, i), 0.0) for i in range(3)]

    def cross(maps_t):
        parts = []
        for j in range(3):
            total = None
            for f in range(FRAMES):
                term = maps_t[j][:, f:f + 1] * centred[j][f:f + 1, :]
                total = term if total is None else total + term
            parts.append(total)
        return blocks(parts[0] + parts[1] + parts[2])

    used = (sub < 3) & first

    def square_mean(maps_t, crosses):
        value = sum(m * c for m, c in zip(maps_t, crosses))
        value = jnp.sum(jnp.where(used, value, 0.0), axis=0, keepdims=True)
        return jnp.sum(value, axis=1, keepdims=True) * (1.0 / atom_count)

    share_of = 1.0 / FRAMES
    m1 = [v * share_of for v in solve(blocks(centred[3]))]
    c1 = cross(m1)
    m2 = [v * share_of for v in solve(c1)]
    c2 = cross(m2)
    variance1 = square_mean(m1, c1) + eps
    variance2 = square_mean(m2, c2) + eps * variance1
    scale = 1.0 / jnp.sqrt(variance2)

    mean_blocks = blocks(jnp.broadcast_to(mean_row, (8, 128)))
    shift = -sum(m * v for m, v in zip(m2, mean_blocks))
    offset = jnp.sum(shift, axis=1, keepdims=True) * scale

    joined = m2[0] + pltpu.roll(m2[1], FRAMES, 1) + pltpu.roll(m2[2], 2 * FRAMES, 1)
    stacked = jnp.concatenate([v.astype(F32) for v in split3(joined)], axis=0).astype(BF16)
    source = iota((128, coord_rows), 1) >> 4
    expand = jnp.where((source % 3) * FRAMES + source // 3 == iota((128, coord_rows), 0), 1.0, 0.0).astype(BF16)
    wide = jnp.dot(stacked, expand, preferred_element_type=F32)
    chunk = iota((8, coord_rows), 1) & (CHUNKS - 1)
    half = iota((8, coord_rows), 0) >> 2
    lhs = jnp.concatenate(
        [jnp.where(chunk == half + 2 * rg, wide[8 * s:8 * s + 8], 0.0) for s in range(3) for rg in range(8)],
        axis=0).astype(BF16)
    def finish(m, side, data):
        base = pl.multiple_of((lax.rem(x + m, 4) * 2 + side) * share, share)
        aligned = jnp.dot(lhs, data, preferred_element_type=F32)
        aligned = aligned[0:64] + aligned[64:128] + aligned[128:192]
        for rg in range(8):
            value = aligned[8 * rg:8 * rg + 8] * scale + offset
            for h in range(2):
                for q in range(lane_tiles):
                    t = q * CHUNKS + 2 * rg + h
                    out[:, pl.ds(pl.multiple_of(base + 128 * t, 128), 128)] = (
                        value[4 * h:4 * h + 3, 128 * q:128 * (q + 1)])

    finish(0, core, z[...])
    for m in range(1, 4):
        finish(m, core, others[m - 1])
    for m in range(4):
        passed[m].wait_recv()
        finish(m, 1 - core, far[m])

    back = FRAMES / jnp.sqrt(variance1)
    entries = [m * back for m in m2] + [shift * back]
    line = jnp.zeros((8, 128), F32)
    for j in range(4):
        value = jnp.sum(jnp.where(lane == frame, entries[j], 0.0), axis=1, keepdims=True)
        line = jnp.where((lane == 4 * sub + j) & (sub < 3), value, line)
    maps[...] = jnp.sum(line, axis=0, keepdims=True)[:, 0:12]

    for copy in exchange + sends + rest + relays + passed:
        copy.wait_send()


def solution(mesh):
    blocks = mesh.shape["atoms"]
    ny = min(8, blocks)
    nz = blocks // ny

    def hbm(value):
        return pltpu.with_memory_space_constraint(value, pltpu.HBM)

    def per_device(coords, start):
        atoms = start.shape[1]
        share = atoms // FRAMES
        width = share // CHUNKS
        dma = pltpu.SemaphoreType.DMA
        return pl.pallas_call(
            functools.partial(kernel, ny, nz),
            out_shape=(
                jax.ShapeDtypeStruct((3, atoms), F32),
                jax.ShapeDtypeStruct((1, 12), F32),
            ),
            in_specs=[pl.BlockSpec(memory_space=pltpu.HBM)] * 2,
            out_specs=(
                pl.BlockSpec(memory_space=pltpu.VMEM),
                pl.BlockSpec(memory_space=pltpu.VMEM),
            ),
            scratch_shapes=[
                pltpu.VMEM((FRAMES, 3, share), BF16),
                pltpu.VMEM((3, share), F32),
                pltpu.VMEM((4 * (share // 128), 128), F32),
                pltpu.VMEM((FRAMES, 3 * CHUNKS, width), BF16),
                pltpu.VMEM((3 * FRAMES * CHUNKS, width), BF16),
                pltpu.VMEM((32 * 8, 2 * width), BF16),
                pltpu.VMEM((3, 3 * FRAMES * CHUNKS, width), BF16),
                pltpu.VMEM((4, 3 * FRAMES * CHUNKS, width), BF16),
                pltpu.VMEM((3, 8, 8, 128), F32),
                dma((FRAMES + 1,)),
                dma((FRAMES - 1,)),
                dma((FRAMES - 1,)),
                dma((3, 8)),
                dma((3, 8)),
                dma((3, FRAMES - 1)),
                dma((3, FRAMES - 1)),
                dma((4,)),
                dma((4,)),
                dma((4,)),
                dma((6,)),
                dma((6,)),
            ],
            compiler_params=pltpu.CompilerParams(
                collective_id=0, has_side_effects=True, vmem_limit_bytes=40 * 1024 * 1024
            ),
        )(hbm(coords), hbm(start))

    return jax.shard_map(
        per_device,
        mesh=mesh,
        in_specs=(P("frames", None, "atoms"), P(None, "atoms")),
        out_specs=(P(None, "atoms"), P("frames", None)),
        check_vma=False,
    )
```
